256 devices in a mesh: seq: 32 (over z, x), pipe: 2 (over core), dp: 4 (over y).
Axes of the slice: x: 4, y: 4, z: 8, core: 2. Of those that a mesh axis runs over, the one named last changes fastest.
Arguments:
- hidden_in: bfloat16 [4, 8192, 1536], P('dp', 'seq'), as said below
- upstream: bfloat16 [4, 8192, 1536], P('dp', 'seq'), as said below
- utt_lengths: int32 [4, 32], P('dp'), may hold values from 1 to 512, 8192 in all within a row
- weight: bfloat16 [2, 1536, 1536], P('pipe'), as said below
- kernel: float32 [2, 32, 1536], P('pipe'), may hold values from -1 to 1
- norm_gain: float32 [2, 1536], P('pipe'), may hold values from 0.1 to 1.9
- norm_bias: float32 [2, 1536], P('pipe'), may hold values from -3 to 3
Outputs:
- grad_input: bfloat16 [4, 8192, 1536], P('dp', 'seq', 'pipe')
- grad_weight: float32 [2, 1536, 1536], P('pipe', ('seq', 'dp'))
- grad_kernel: float32 [2, 32, 1536], P('pipe')
- grad_gain: float32 [2, 1536], P('pipe')
- grad_bias: float32 [2, 1536], P('pipe')
The draws below stay inside these ranges and needn't reach their ends.
Inputs may be any that keep to these rules, and one draw needn't show every extreme that they name: `utt_lengths`: each bin's lengths sum to 8192; the longest utterance of every bin has exactly 512 frames. `hidden_in`: frame scales vary from frame to frame. `upstream`: entries of order one. `weight`: entries of order one over the square root of 1536.
All inputs are finite; a program needn't handle non-finite values.
Results may differ from the reference program's by a relative error of at most 0.019.
Values may be sent and summed in bfloat16 or wider, within the bound.
A program may use at most 128 MiB of HBM per device.

```python
import math
import jax
import jax.numpy as jnp
import numpy as np
from jax import lax

D = 1536
KERNEL = 32
TOK_DEV = 256
SECTIONS = 2
BINS = 4
LENGTH = 8192
UTTS = 32
MOST = 512


def shared_signs(key):
    sign_key = jax.random.fold_in(key, 5)
    sign_bits = jax.random.randint(sign_key, (D,), 0, 2)
    return (2 * sign_bits - 1).astype(jnp.float32)


def draw_hidden_in(key, part):
    key = jax.random.fold_in(key, 11)
    key_values, key_scale = jax.random.split(key, 2)
    positions = jnp.arange(LENGTH, dtype=jnp.float32) / LENGTH
    roughness = jnp.exp(jax.random.uniform(key_scale, (BINS, LENGTH, 1), jnp.float32, jnp.log(0.5), jnp.log(5.0)))
    values = jax.random.normal(key_values, (BINS, LENGTH, D), jnp.float32)
    trend_line = 1.0 + 2.0 * positions
    return (values * roughness * trend_line[None, :, None]).astype(jnp.bfloat16)


def draw_weight(key, part):
    signs = shared_signs(key)
    key = jax.random.fold_in(key, 13)
    base = jnp.clip(jax.random.normal(key, (SECTIONS, D, D), jnp.float32), -4.0, 4.0)
    values = base * D ** (-0.5) + 8.0 / D * signs[None, None, :]
    return values.astype(jnp.bfloat16)


def draw_upstream(key, part):
    signs = shared_signs(key)
    key = jax.random.fold_in(key, 17)
    key_noise, key_phase = jax.random.split(key, 2)
    frames = jnp.arange(LENGTH, dtype=jnp.float32)
    phase = jax.random.uniform(key_phase, (BINS, 1), jnp.float32, 0.0, 2.0 * math.pi)
    noise = jnp.clip(jax.random.normal(key_noise, (BINS, LENGTH, D), jnp.float32), -5.0, 5.0)
    period = 3.0 * TOK_DEV
    height = 0.3
    wave = height * jnp.sin(2.0 * math.pi * frames[None, :] / period + phase)
    return (noise + wave[:, :, None] * signs[None, None, :]).astype(jnp.bfloat16)


def block_levels(key, dims, shards, least, top_value):
    factor_of, own = 1.0, jax.random.fold_in(key, 6)
    for dim, parts in shards:
        heights = jnp.exp(jax.random.uniform(jax.random.fold_in(own, dim), (parts,), jnp.float32, least / len(shards), top_value / len(shards)))
        factor_of = factor_of * jnp.repeat(heights, dims[dim] // parts).reshape([-1 if axis == dim else 1 for axis in range(len(dims))])
    return factor_of


def profile(amount, total, limit, slope):
    loads = [(1 << 20) // math.isqrt(rank ** slope) + 1 for rank in range(2, amount + 1)]
    rest, given = total - limit - (amount - 1), [1] * (amount - 1)
    while rest > 0:
        movable = [i for i in range(amount - 1) if given[i] < limit]
        whole, left = sum([loads[i] for i in movable]), rest
        for i in movable:
            addition = min(limit - given[i], max(1, left * loads[i] // whole), rest)
            given[i] = given[i] + addition
            rest = rest - addition
    return np.array([limit] + given)


def ragged(own_key, amount, total, reach, lean):
    if amount == 2:
        one = jax.random.randint(own_key, (), max(1, total - reach), min(reach, total - 1) + 1)
        return jnp.stack([one, total - one])
    sizes = jnp.asarray(profile(amount, total, reach, lean), jnp.int32)
    couples = (amount - 1) // 2
    source_of, receiver = sizes[1:1 + 2 * couples:2], sizes[2:2 + 2 * couples:2]
    margin = jnp.minimum(source_of - 1, reach - receiver)
    shifted = jax.random.randint(jax.random.fold_in(own_key, 1), (couples,), 0, 1 << 20) % (margin + 1)
    sizes = sizes.at[1:1 + 2 * couples:2].set(source_of - shifted).at[2:2 + 2 * couples:2].set(receiver + shifted)
    return sizes[jax.random.permutation(jax.random.fold_in(own_key, 2), amount)]


def bell_draw(stream_key, shape, deviation, bound, cuts=(), held_as=jnp.bfloat16):
    level = block_levels(stream_key, shape, cuts, -0.22, 0.18) if cuts else 1.0
    drawn = jax.random.normal(stream_key, shape, jnp.float32) * deviation * level
    return jnp.minimum(jnp.maximum(drawn, -bound), bound).astype(held_as)


def setup_inputs(seed: int = 0) -> dict:
    key_list = jax.random.split(jax.random.key(seed), 8)
    return {
        "hidden_in": draw_hidden_in(jax.random.fold_in(key_list[7], 71), 0),
        "upstream": draw_upstream(jax.random.fold_in(key_list[7], 71), 0),
        "utt_lengths": jax.vmap(lambda own: ragged(own, UTTS, LENGTH, MOST, 2))(jax.random.split(key_list[2], BINS)).reshape((BINS, UTTS)).astype(jnp.int32),
        "weight": draw_weight(jax.random.fold_in(key_list[7], 71), 0),
        "kernel": bell_draw(key_list[4], (SECTIONS, KERNEL, D), KERNEL ** -0.5, 1.0, ((0, 2),), jnp.float32),
        "norm_gain": jnp.clip(1.0 + 0.18 * jax.random.normal(key_list[5], (SECTIONS, D), jnp.float32), 0.1, 1.9),
        "norm_bias": bell_draw(key_list[6], (SECTIONS, D), 0.5, 3.0, ((0, 2),), jnp.float32),
    }


EPSILON = 1e-05
HIGHEST = lax.Precision.HIGHEST

def frame_ids(lengths, first_frame, frame_count):
    starts = (jnp.cumsum(lengths) - lengths).astype(jnp.int32)
    frames = (first_frame + jnp.arange(frame_count, dtype=jnp.int32)).astype(jnp.int32)
    owners = lax.optimization_barrier(jnp.sum((starts[None, :] <= frames[:, None]).astype(jnp.int32), axis=1)) - 1
    bin_total = jnp.sum(lengths).astype(jnp.int32)
    inside = (frames >= 0) & (frames < bin_total)
    return jnp.where(inside, owners, -2).astype(jnp.int32)

def depthwise(padded, padded_seg, kernel, frame_rows):
    tap_count = kernel.shape[0]
    centre = padded_seg[tap_count // 2:tap_count // 2 + frame_rows]
    result = jnp.zeros((frame_rows, padded.shape[1]), jnp.float32)
    for tap_index in range(tap_count):
        window = padded[tap_index + 1:tap_index + 1 + frame_rows].astype(jnp.float32)
        same_utt = (padded_seg[tap_index + 1:tap_index + 1 + frame_rows] == centre)[:, None]
        result = result + jnp.where(same_utt, window * kernel[tap_index][None, :], 0.0)
    return result

def depthwise_back(padded_grad, padded_seg, kernel, frame_rows):
    tap_count = kernel.shape[0]
    centre = padded_seg[tap_count // 2:tap_count // 2 + frame_rows]
    result = jnp.zeros((frame_rows, padded_grad.shape[1]), jnp.float32)
    for tap_index in range(tap_count):
        offset = tap_count - 1 - tap_index
        window = padded_grad[offset:offset + frame_rows].astype(jnp.float32)
        same_utt = (padded_seg[offset:offset + frame_rows] == centre)[:, None]
        result = result + jnp.where(same_utt, window * kernel[tap_index][None, :], 0.0)
    return result

def kernel_grad(padded, padded_seg, conv_grad, frame_rows, tap_count):
    centre = padded_seg[tap_count // 2:tap_count // 2 + frame_rows]
    grad_float = conv_grad.astype(jnp.float32)
    pieces = []
    for tap_index in range(tap_count):
        window = padded[tap_index + 1:tap_index + 1 + frame_rows].astype(jnp.float32)
        same_utt = (padded_seg[tap_index + 1:tap_index + 1 + frame_rows] == centre)[:, None]
        pieces.append(lax.optimization_barrier(jnp.sum(jnp.where(same_utt, window * grad_float, 0.0), axis=0)))
    return jnp.stack(pieces)

def section_forward(hidden, lengths, kernel, gain, bias, weight):
    frame_rows, model_width = hidden.shape
    rim_width = kernel.shape[0] // 2
    padded = jnp.pad(hidden, ((rim_width, rim_width), (0, 0)))
    padded_seg = frame_ids(lengths, -rim_width, frame_rows + 2 * rim_width)
    frame_seg = padded_seg[rim_width:rim_width + frame_rows]
    conv_out = depthwise(padded, padded_seg, kernel, frame_rows)
    onehot = (frame_seg[:, None] == jnp.arange(lengths.shape[0], dtype=jnp.int32)[None, :]).astype(jnp.float32)
    stacked = jnp.stack([lax.optimization_barrier(jnp.sum(conv_out, axis=1)), lax.optimization_barrier(jnp.sum(conv_out * conv_out, axis=1))])
    utt_table = jnp.dot(stacked, onehot, precision=HIGHEST)
    counts = lengths.astype(jnp.float32) * model_width
    means_utt = utt_table[0] / counts
    spread = utt_table[1] / counts - means_utt * means_utt
    inv_scale = lax.rsqrt(spread + EPSILON)
    frame_stats = jnp.dot(onehot, jnp.stack([means_utt, inv_scale], axis=1), precision=HIGHEST)
    normed = (conv_out - frame_stats[:, 0:1]) * frame_stats[:, 1:2]
    pre_act = normed * gain[None, :] + bias[None, :]
    activation = jax.nn.silu(pre_act).astype(jnp.bfloat16)
    product = jnp.dot(activation, weight, preferred_element_type=jnp.float32)
    output = (hidden.astype(jnp.float32) + product).astype(jnp.bfloat16)
    return (output, (padded, padded_seg, onehot, frame_stats, normed, pre_act, activation))

def section_backward(upstream_grad, saved_forward, lengths, kernel, gain, weight):
    padded, padded_seg, onehot, frame_stats, normed, pre_act, activation = saved_forward
    frame_rows, model_width = upstream_grad.shape
    rim_width = kernel.shape[0] // 2
    act_grad = lax.dot_general(upstream_grad, weight, (((1,), (1,)), ((), ())), preferred_element_type=jnp.float32)
    sigmoid_out = jax.nn.sigmoid(pre_act)
    pre_grad = act_grad * sigmoid_out * (1.0 + pre_act * (1.0 - sigmoid_out))
    normed_grad = pre_grad * gain[None, :]
    stacked = jnp.stack([lax.optimization_barrier(jnp.sum(normed_grad, axis=1)), lax.optimization_barrier(jnp.sum(normed_grad * normed, axis=1))])
    utt_table = jnp.dot(stacked, onehot, precision=HIGHEST)
    counts = lengths.astype(jnp.float32) * model_width
    per_frame = jnp.dot(onehot, (utt_table / counts[None, :]).T, precision=HIGHEST)
    conv_grad = (frame_stats[:, 1:2] * (normed_grad - per_frame[:, 0:1] - normed * per_frame[:, 1:2])).astype(jnp.bfloat16)
    padded_grad = jnp.pad(conv_grad, ((rim_width, rim_width), (0, 0)))
    input_grad = (upstream_grad.astype(jnp.float32) + depthwise_back(padded_grad, padded_seg, kernel, frame_rows)).astype(jnp.bfloat16)
    weight_part = jnp.dot(activation.T, upstream_grad, preferred_element_type=jnp.float32)
    kernel_part = kernel_grad(padded, padded_seg, conv_grad, frame_rows, kernel.shape[0])
    gain_part = lax.optimization_barrier(jnp.sum(pre_grad * normed, axis=0))
    bias_part = lax.optimization_barrier(jnp.sum(pre_grad, axis=0))
    return (input_grad, (weight_part, kernel_part, gain_part, bias_part))

def reference(hidden_in, upstream, utt_lengths, weight, kernel, norm_gain, norm_bias):
    section_total = weight.shape[0]

    def one_bin(inputs):
        hidden, cotangent, lengths = inputs
        saved_list = []
        section_input = hidden
        for section_index in range(section_total):
            section_output, fresh_saved = section_forward(section_input, lengths, kernel[section_index], norm_gain[section_index], norm_bias[section_index], weight[section_index])
            saved_list.append(fresh_saved)
            section_input = section_output
        upstream_grad = cotangent
        grads_list = [None] * section_total
        for section_index in range(section_total - 1, -1, -1):
            upstream_grad, grads_list[section_index] = section_backward(upstream_grad, saved_list[section_index], lengths, kernel[section_index], norm_gain[section_index], weight[section_index])
        stacked = tuple((jnp.stack([grads_list[k][m] for k in range(section_total)]) for m in range(4)))
        return (upstream_grad, stacked)
    input_grads, per_bin = lax.map(one_bin, (hidden_in, upstream, utt_lengths))
    grad_weight = lax.optimization_barrier(jnp.sum(per_bin[0], axis=0))
    grad_kernel = lax.optimization_barrier(jnp.sum(per_bin[1], axis=0))
    grad_gain = lax.optimization_barrier(jnp.sum(per_bin[2], axis=0))
    grad_bias = lax.optimization_barrier(jnp.sum(per_bin[3], axis=0))
    return (input_grads, grad_weight, grad_kernel, grad_gain, grad_bias)
```

```python
import types

import jax
import jax.numpy as jnp
from jax import lax
from jax.experimental import pallas as pl
from jax.experimental.pallas import tpu as pltpu
from jax.sharding import PartitionSpec as P

EPSILON = 1e-05
MESH = pl.DeviceIdType.MESH
F32, BF16 = jnp.float32, jnp.bfloat16
D, HALF, ROWS, TAPS, RIM, UTTS = 1536, 768, 256, 32, 16, 32
LANE, TILES = 128, 6
NX, NY, NZ = 4, 4, 8
SEQ = NX * NZ
BLOCK = 12
STEP, GROUP = 32, 3
PADDED = ROWS + 2 * RIM

PLANE = [(dx, dy) for dx in range(NX) for dy in range(NY)]
OFFSETS = [(s, rel) for s in (-2, -1, 0, 1, 2) for rel in (0, 1) if (s, rel) != (0, 0)]
GATHER = [(dx, dy, rel) for dx, dy in PLANE for rel in (0, 1) if (dx, dy, rel) != (0, 0, 0)]


def scratch():
    vm, dma = pltpu.VMEM, pltpu.SemaphoreType.DMA
    return dict(
        hb=vm((ROWS, HALF), BF16),
        gbuf=vm((2, 2, ROWS, HALF), BF16),
        w=vm((2, HALF, D), BF16),
        pst=vm((2, TILES, 40, LANE), F32),
        pb=vm((2, TILES, 40, LANE), F32),
        seg=vm((PADDED, LANE), F32),
        cnt=vm((8, LANE), F32),
        perm=vm((2, HALF, HALF), BF16),
        xf=vm((2, TILES, PADDED, LANE), F32),
        y=vm((2, TILES, ROWS, LANE), F32),
        inv=vm((2, ROWS, LANE), F32),
        act=vm((2, ROWS, HALF), BF16),
        ag=vm((ROWS, HALF), F32),
        cg=vm((TILES, PADDED, LANE), F32),
        kga=vm((TILES, TAPS, 8, LANE), F32),
        gba=vm((2, 2, TILES, 8, LANE), F32),
        halo=vm((4, 2, RIM, HALF), BF16),
        edge=vm((2, 2, RIM, HALF), BF16),
        hx=vm((2, ROWS, HALF), BF16),
        h1=vm((ROWS, HALF), BF16),
        tab=vm((4, 8, LANE), F32),
        tabr=vm((4, 9, 8, LANE), F32),
        gwb=vm((2, 2, HALF, HALF), BF16),
        r1=vm((2, 2, 3, HALF // 4, HALF), BF16),
        s2=vm((2, 2, HALF // 4, HALF), BF16),
        r2=vm((2, 2, 3, HALF // 16, HALF), BF16),
        t3=vm((HALF // 16 + 8, HALF), F32),
        s3=vm((2, 4, 2, 16, HALF), BF16),
        r3=vm((NZ, 2, 16, HALF), BF16),
        sb=vm((16, 32, LANE), F32),
        ar=vm((15, 32, LANE), F32),
        zb=vm((NZ, 32, LANE), F32),
        fs=vm((2, 16, LANE), F32),
        fin=vm((2, 16, 16, LANE), F32),
        lsem=dma((4,)),
        hs=dma((4, 2)), hr=dma((4, 2)),
        ws=dma((2,)), wr=dma((2,)),
        xs=dma((2,)), xr=dma((2,)),
        ts=dma((4, 9)), tr=dma((4, 9)),
        s1s=dma((2, 2, 3)), s1r=dma((2, 2, 3)),
        s2s=dma((2, 2, 3)), s2r=dma((2, 2, 3)),
        s3s=dma((2, 4)), s3r=dma((NZ,)),
        as_=dma((15,)), ar_=dma((15,)),
        zs=dma((7,)), zr=dma((7,)),
        gs=dma((31,)), gr=dma((31,)),
    )


def fold(v):
    total = v[0:8]
    for r in range(8, v.shape[0], 8):
        total = total + v[r : r + 8]
    return total


def dot(a, b):
    return jnp.dot(a, b, preferred_element_type=F32)


def dot_t(a, b):
    return lax.dot_general(a, b, (((1,), (1,)), ((), ())), preferred_element_type=F32)


def cols(c):
    return slice(c * LANE, (c + 1) * LANE)


def main_kernel(names, hid, up, len_ref, w_hbm, ker_ref, gain_ref, bias_ref,
                gi_ref, gw_ref, gk_ref, gg_ref, gb_ref, *refs):
    S = types.SimpleNamespace(**dict(zip(names, refs)))
    i, p, y = lax.axis_index("seq"), lax.axis_index("pipe"), lax.axis_index("dp")
    q = 1 - p
    z, x = lax.div(i, NX), lax.rem(i, NX)
    own_col = pl.multiple_of(p * HALF, HALF)
    oth_col = pl.multiple_of(q * HALF, HALF)

    def dev(seq, pipe, dp):
        return {"seq": seq, "pipe": pipe, "dp": dp}

    def along(offset, pipe):
        return dev(lax.rem(i + offset + SEQ, SEQ), pipe, y)

    def plane(dx, dy, pipe):
        return dev(z * NX + lax.rem(x + dx, NX), pipe, lax.rem(y + dy, NY))

    def depth(dz, pipe):
        return dev(lax.rem(z + dz, NZ) * NX + x, pipe, y)

    core = (p, q)
    sends = []

    def push(src, dst, ssem, rsem, target):
        copy = pltpu.make_async_remote_copy(
            src_ref=src, dst_ref=dst, send_sem=ssem, recv_sem=rsem,
            device_id=target, device_id_type=MESH,
        )
        copy.start()
        sends.append(copy)
        return copy

    loc = [
        pltpu.make_async_copy(hid.at[0, :, pl.ds(own_col, HALF)], S.hb, S.lsem.at[0]),
        pltpu.make_async_copy(w_hbm.at[0, pl.ds(own_col, HALF), :], S.w.at[p], S.lsem.at[1]),
        pltpu.make_async_copy(up.at[0, :, pl.ds(0, HALF)], S.gbuf.at[1, 0], S.lsem.at[2]),
        pltpu.make_async_copy(up.at[0, :, pl.ds(HALF, HALF)], S.gbuf.at[1, 1], S.lsem.at[3]),
    ]
    for copy in loc:
        copy.start()

    barrier = pltpu.get_barrier_semaphore()
    partners = [along(s, core[rel]) for s, rel in OFFSETS]
    partners += [plane(dx, dy, c) for dx, dy in PLANE if (dx, dy) != (0, 0) for c in core]
    partners += [depth(dz, c) for dz in range(1, NZ) for c in core]
    for target in partners:
        pl.semaphore_signal(barrier, inc=1, device_id=target, device_id_type=MESH)

    for h in range(2):
        for c in range(TILES):
            at = slice(h * HALF + c * LANE, h * HALF + (c + 1) * LANE)
            S.pst[h, c, 0:TAPS, :] = ker_ref[0, :, at]
            row = lax.broadcasted_iota(jnp.int32, (8, LANE), 0)
            S.pst[h, c, TAPS:40, :] = jnp.where(
                row == 0, gain_ref[:, at], jnp.where(row == 1, bias_ref[:, at], 0.0)
            )
    for c in range(TILES):
        S.pb[p, c] = S.pst[p, c]

    lens = len_ref[...].astype(F32)
    io0 = lax.broadcasted_iota(jnp.int32, (UTTS, UTTS), 0)
    io1 = lax.broadcasted_iota(jnp.int32, (UTTS, UTTS), 1)
    lens_col = jnp.sum(jnp.where(io0 == io1, lens, 0.0), axis=1, keepdims=True)
    starts = jnp.sum(jnp.where(io0 < io1, lens_col, 0.0), axis=0, keepdims=True)
    bin_total = jnp.sum(lens, axis=1, keepdims=True)
    frame = (lax.broadcasted_iota(jnp.int32, (PADDED, UTTS), 0) + (i * ROWS - RIM)).astype(F32)
    owner = jnp.sum(jnp.where(starts <= frame, 1.0, 0.0), axis=1, keepdims=True) - 1.0
    inside = (frame[:, 0:1] >= 0.0) & (frame[:, 0:1] < bin_total)
    S.seg[...] = jnp.broadcast_to(jnp.where(inside, owner, -2.0), (PADDED, LANE))
    S.cnt[...] = jnp.full((8, LANE), float(D), F32)
    S.cnt[0:1, 0:UTTS] = lens * float(D)

    r = lax.broadcasted_iota(jnp.int32, (HALF, LANE), 0).astype(F32)
    blk = jnp.floor((r + 0.5) / BLOCK)
    word = r - BLOCK * blk
    b4 = jnp.floor((blk + 0.5) / 4.0)
    dig0 = blk - 4.0 * b4
    dig2 = jnp.floor((b4 + 0.5) / 4.0)
    dig1 = b4 - 4.0 * dig2
    lane = lax.broadcasted_iota(jnp.int32, (HALF, LANE), 1).astype(F32)
    for path, (yy, xx) in enumerate(((dig2, dig1), (dig1, dig2))):
        nat = ((dig0 * 4.0 + xx) * 4.0 + yy) * BLOCK + word
        for c in range(TILES):
            S.perm[path, :, cols(c)] = jnp.where(nat == lane + float(c * LANE), 1.0, 0.0).astype(BF16)

    S.kga[...] = jnp.zeros(S.kga.shape, F32)
    S.sb[15] = jnp.zeros((32, LANE), F32)
    S.t3[HALF // 16 :, :] = jnp.zeros((8, HALF), F32)

    pl.semaphore_wait(barrier, len(partners))

    def send_halo(rnd, first, last):
        return [
            push(last, S.halo.at[rnd, 0], S.hs.at[rnd, 0], S.hr.at[rnd, 0], along(1, p)),
            push(first, S.halo.at[rnd, 1], S.hs.at[rnd, 1], S.hr.at[rnd, 1], along(-1, p)),
        ]

    def take_halo(rnd, copies, dst):
        for copy in copies:
            copy.wait_recv()
        for c in range(TILES):
            dst[c, 0:RIM, :] = S.halo[rnd, 0, :, cols(c)].astype(F32)
            dst[c, RIM + ROWS :, :] = S.halo[rnd, 1, :, cols(c)].astype(F32)

    halo_copies = send_halo(
        0,
        hid.at[0, pl.ds(0, RIM), pl.ds(own_col, HALF)],
        hid.at[0, pl.ds(ROWS - RIM, RIM), pl.ds(own_col, HALF)],
    )
    par_copy = push(S.pst.at[q], S.pb.at[p], S.ws.at[0], S.wr.at[0], along(0, q))
    w_copy = push(
        w_hbm.at[0, pl.ds(oth_col, HALF), :], S.w.at[p], S.ws.at[1], S.wr.at[1], along(0, q)
    )

    loc[0].wait()
    for c in range(TILES):
        S.xf[0, c, RIM : RIM + ROWS, :] = S.hb[:, cols(c)].astype(F32)

    steps = ROWS // STEP
    lane_id = lax.broadcasted_iota(jnp.int32, (STEP, LANE), 1).astype(F32)

    def base_of(b):
        return pl.multiple_of(b * STEP, STEP)

    def member(base):
        return S.seg[pl.ds(base + RIM, STEP), :] == lane_id

    def table_add(onehot, v):
        return fold(jnp.where(onehot, jnp.sum(v, axis=1, keepdims=True), 0.0))

    def pick(onehot, row):
        return jnp.sum(jnp.where(onehot, row, 0.0), axis=1, keepdims=True)

    zero_tab = jnp.zeros((8, LANE), F32)

    def send_table(rnd, t1, t2):
        row = lax.broadcasted_iota(jnp.int32, (8, LANE), 0)
        t1 = jnp.sum(t1, axis=0, keepdims=True)
        t2 = jnp.sum(t2, axis=0, keepdims=True)
        S.tab[rnd] = jnp.where(row == 0, t1, jnp.where(row == 1, t2, 0.0))
        return [
            push(S.tab.at[rnd], S.tabr.at[rnd, n], S.ts.at[rnd, n], S.tr.at[rnd, n], along(s, core[rel]))
            for n, (s, rel) in enumerate(OFFSETS)
        ]

    def take_table(rnd, copies):
        total = S.tab[rnd]
        for copy in copies:
            copy.wait_recv()
        for n in range(9):
            total = total + S.tabr[rnd, n]
        count = S.cnt[0:1, :]
        return total[0:1] / count, total[1:2] / count

    def conv_forward(s):
        def step(b, carry):
            t1, t2 = carry
            base = base_of(b)
            centre = S.seg[pl.ds(base + RIM, STEP), :]
            first = second = jnp.zeros((STEP, LANE), F32)
            for g in range(0, TILES, GROUP):
                acc = [jnp.zeros((STEP, LANE), F32) for _ in range(GROUP)]
                for j in range(TAPS):
                    same = S.seg[pl.ds(base + j + 1, STEP), :] == centre
                    for c in range(GROUP):
                        window = S.xf[s, g + c, pl.ds(base + j + 1, STEP), :]
                        acc[c] = acc[c] + jnp.where(same, window * S.pb[s, g + c, j : j + 1, :], 0.0)
                for c in range(GROUP):
                    S.y[s, g + c, pl.ds(base, STEP), :] = acc[c]
                    first = first + acc[c]
                    second = second + acc[c] * acc[c]
            onehot = member(base)
            return t1 + table_add(onehot, first), t2 + table_add(onehot, second)

        return lax.fori_loop(0, steps, step, (zero_tab, zero_tab))

    def moments(rnd, copies):
        mean, square = take_table(rnd, copies)
        spread = jnp.maximum(square - mean * mean, 0.0)
        return mean, lax.rsqrt(spread + EPSILON)

    def normalize(s, base, onehot, mean, scale):
        m, v = pick(onehot, mean), pick(onehot, scale)
        S.inv[s, pl.ds(base, STEP), :] = jnp.broadcast_to(v, (STEP, LANE))
        return m, v

    def activate(s, base, c, normed):
        gain, bias = S.pb[s, c, TAPS : TAPS + 1, :], S.pb[s, c, TAPS + 1 : TAPS + 2, :]
        pre = normed * gain + bias
        sig = jax.nn.sigmoid(pre)
        return gain, pre, sig

    take_halo(0, halo_copies, S.xf.at[0])
    par_copy.wait_recv()
    copies = send_table(0, *conv_forward(0))
    mean, scale = moments(0, copies)

    def norm_step(b, _):
        base = base_of(b)
        m, v = normalize(0, base, member(base), mean, scale)
        for c in range(TILES):
            normed = (S.y[0, c, pl.ds(base, STEP), :] - m) * v
            S.y[0, c, pl.ds(base, STEP), :] = normed
            _, pre, sig = activate(0, base, c, normed)
            S.act[0, pl.ds(base, STEP), cols(c)] = (pre * sig).astype(BF16)
        return 0

    lax.fori_loop(0, steps, norm_step, 0)
    loc[1].wait()
    w_copy.wait_recv()
    S.hx[0] = dot(S.act[0], S.w[0, :, pl.ds(oth_col, HALF)]).astype(BF16)
    copy = push(S.hx.at[0], S.hx.at[1], S.xs.at[0], S.xr.at[0], along(0, q))
    S.ag[...] = dot(S.act[0], S.w[0, :, pl.ds(own_col, HALF)])
    copy.wait_recv()

    def out_step(b, _):
        base = base_of(b)
        at = pl.ds(base, STEP)
        S.h1[at, :] = (S.hb[at, :].astype(F32) + (S.ag[at, :] + S.hx[1, at, :].astype(F32))).astype(BF16)
        return 0

    lax.fori_loop(0, steps, out_step, 0)
    halo_copies = send_halo(1, S.h1.at[pl.ds(0, RIM), :], S.h1.at[pl.ds(ROWS - RIM, RIM), :])
    for c in range(TILES):
        S.xf[1, c, RIM : RIM + ROWS, :] = S.h1[:, cols(c)].astype(F32)
    take_halo(1, halo_copies, S.xf.at[1])

    copies = send_table(1, *conv_forward(1))

    def act_grad(s):
        S.ag[...] = dot_t(S.gbuf[s, 0], S.w[s, :, 0:HALF]) + dot_t(S.gbuf[s, 1], S.w[s, :, HALF:])

    loc[2].wait()
    loc[3].wait()
    act_grad(1)
    mean, scale = moments(1, copies)

    def pre_grad(s, mean, scale):
        def step(b, carry):
            t1, t2, gains, biases = carry
            base = base_of(b)
            onehot = member(base)
            at = pl.ds(base, STEP)
            if s == 1:
                m, v = normalize(1, base, onehot, mean, scale)
            first = second = jnp.zeros((STEP, LANE), F32)
            new_gains, new_biases = [], []
            for c in range(TILES):
                normed = S.y[s, c, at, :]
                if s == 1:
                    normed = (normed - m) * v
                    S.y[1, c, at, :] = normed
                gain, pre, sig = activate(s, base, c, normed)
                if s == 1:
                    S.act[1, at, cols(c)] = (pre * sig).astype(BF16)
                grad = S.ag[at, cols(c)] * sig * (1.0 + pre * (1.0 - sig))
                scaled = grad * gain
                S.ag[at, cols(c)] = scaled
                first = first + scaled
                second = second + scaled * normed
                new_gains.append(gains[c] + fold(grad * normed))
                new_biases.append(biases[c] + fold(grad))
            return (t1 + table_add(onehot, first), t2 + table_add(onehot, second),
                    tuple(new_gains), tuple(new_biases))

        zeros = tuple(zero_tab for _ in range(TILES))
        t1, t2, gains, biases = lax.fori_loop(0, steps, step, (zero_tab, zero_tab, zeros, zeros))
        for c in range(TILES):
            S.gba[s, 0, c] = gains[c]
            S.gba[s, 1, c] = biases[c]
        return t1, t2

    def conv_grad(s, rnd, copies):
        mean_a, mean_b = take_table(rnd, copies)

        def step(b, _):
            base = base_of(b)
            onehot = member(base)
            ca, cb = pick(onehot, mean_a), pick(onehot, mean_b)
            at = pl.ds(base, STEP)
            v = S.inv[s, at, :]
            for c in range(TILES):
                S.cg[c, pl.ds(base + RIM, STEP), :] = v * (S.ag[at, cols(c)] - ca - S.y[s, c, at, :] * cb)
            return 0

        lax.fori_loop(0, steps, step, 0)
        for c in range(TILES):
            S.edge[s, 0, :, cols(c)] = S.cg[c, RIM : 2 * RIM, :].astype(BF16)
            S.edge[s, 1, :, cols(c)] = S.cg[c, ROWS : ROWS + RIM, :].astype(BF16)
        return send_halo(rnd, S.edge.at[s, 0], S.edge.at[s, 1])

    def conv_backward(s):
        def step(b, _):
            base = base_of(b)
            at = pl.ds(base, STEP)
            centre = S.seg[pl.ds(base + RIM, STEP), :]
            for g in range(0, TILES, GROUP):
                acc = [jnp.zeros((STEP, LANE), F32) for _ in range(GROUP)]
                mine = [S.xf[s, g + c, pl.ds(base + RIM, STEP), :] for c in range(GROUP)]
                for j in range(TAPS):
                    same = S.seg[pl.ds(base + TAPS - 1 - j, STEP), :] == centre
                    for c in range(GROUP):
                        window = jnp.where(same, S.cg[g + c, pl.ds(base + TAPS - 1 - j, STEP), :], 0.0)
                        acc[c] = acc[c] + window * S.pb[s, g + c, j : j + 1, :]
                        S.kga[g + c, j] += fold(window * mine[c])
                for c in range(GROUP):
                    passed = S.gbuf[s, p, at, cols(g + c)].astype(F32) + acc[c]
                    if s == 1:
                        S.gbuf[0, p, at, cols(g + c)] = passed.astype(BF16)
                    else:
                        gi_ref[0, at, cols(g + c)] = passed.astype(BF16)
            return 0

        lax.fori_loop(0, steps, step, 0)

    def keep_small(s):
        row = lax.broadcasted_iota(jnp.int32, (8, LANE), 0)
        for c in range(TILES):
            for k in range(4):
                t = c * 5 + k
                at = slice(s * 16 + (t % 2) * 8, s * 16 + (t % 2) * 8 + 8)
                S.sb[t // 2, at, :] = jnp.sum(S.kga[c, 8 * k : 8 * k + 8], axis=1)
            t = c * 5 + 4
            at = slice(s * 16 + (t % 2) * 8, s * 16 + (t % 2) * 8 + 8)
            gsum = jnp.sum(S.gba[s, 0, c], axis=0, keepdims=True)
            bsum = jnp.sum(S.gba[s, 1, c], axis=0, keepdims=True)
            S.sb[t // 2, at, :] = jnp.where(row == 0, gsum, jnp.where(row == 1, bsum, 0.0))

    def weight_partial(s):
        def step(k, _):
            at = pl.ds(pl.multiple_of(k * 256, 256), 256)
            for path in range(2):
                turned = dot_t(S.perm[path, at, :], S.act[s]).astype(BF16)
                S.gwb[s, path, at, :] = dot(turned, S.gbuf[s, path]).astype(BF16)
            return 0

        lax.fori_loop(0, HALF // 256, step, 0)

    def ring_target(path, d):
        return plane(0, d, p) if path == 0 else plane(d, 0, p)

    def ring_index(path, d):
        return lax.rem((y if path == 0 else x) + d, 4)

    q1, q2 = HALF // 4, HALF // 16

    def first_exchange(s):
        return [
            push(
                S.gwb.at[s, path, pl.ds(pl.multiple_of(ring_index(path, d) * q1, q1), q1), :],
                S.r1.at[s, path, d - 1], S.s1s.at[s, path, d - 1], S.s1r.at[s, path, d - 1],
                ring_target(path, d),
            )
            for d in (1, 2, 3) for path in range(2)
        ]

    def second_exchange(s, copies):
        for copy in copies:
            copy.wait_recv()
        for path in range(2):
            def step(k, _):
                at = pl.ds(pl.multiple_of(k * 48, 48), 48)
                mine = pl.ds(pl.multiple_of(ring_index(path, 0) * q1 + k * 48, 48), 48)
                total = S.gwb[s, path, mine, :].astype(F32)
                for d in range(3):
                    total = total + S.r1[s, path, d, at, :].astype(F32)
                S.s2[s, path, at, :] = total.astype(BF16)
                return 0

            lax.fori_loop(0, 4, step, 0)
        return [
            push(
                S.s2.at[s, path, pl.ds(pl.multiple_of(ring_index(1 - path, d) * q2, q2), q2), :],
                S.r2.at[s, path, d - 1], S.s2s.at[s, path, d - 1], S.s2r.at[s, path, d - 1],
                ring_target(1 - path, d),
            )
            for d in (1, 2, 3) for path in range(2)
        ]

    near = lax.div(z, 4) == p

    def third_exchange(s, copies):
        for copy in copies:
            copy.wait_recv()
        for path in range(2):
            mine = pl.ds(pl.multiple_of(ring_index(1 - path, 0) * q2, q2), q2)
            total = S.s2[s, path, mine, :].astype(F32)
            for d in range(3):
                total = total + S.r2[s, path, d].astype(F32)
            S.t3[0:q2, :] = total
            for k in range(4):
                S.s3[s, k, path] = S.t3[BLOCK * k : BLOCK * k + 16, :].astype(BF16)
        for k in range(4):
            target_z = 4 * p + k
            stays = (target_z == z) & (p == s)
            copy = pltpu.make_async_remote_copy(
                src_ref=S.s3.at[s, k], dst_ref=S.r3.at[z], send_sem=S.s3s.at[s, k],
                recv_sem=S.s3r.at[z], device_id=dev(target_z * NX + x, s, y), device_id_type=MESH,
            )

            @pl.when(jnp.logical_not(stays))
            def _():
                copy.start()

            @pl.when(stays)
            def _():
                S.r3[z] = S.s3[s, k]

    def finish_third():
        for s in range(2):
            for k in range(4):
                target_z = 4 * p + k
                stays = (target_z == z) & (p == s)

                @pl.when(jnp.logical_not(stays))
                def _():
                    pltpu.make_async_remote_copy(
                        src_ref=S.s3.at[s, k], dst_ref=S.r3.at[z], send_sem=S.s3s.at[s, k],
                        recv_sem=S.s3r.at[z], device_id=dev(target_z * NX + x, s, y),
                        device_id_type=MESH,
                    ).wait_send()
        for k in range(NZ):
            @pl.when(jnp.logical_not((z == k) & near))
            def _():
                pltpu.make_async_remote_copy(
                    src_ref=S.s3.at[0, 0], dst_ref=S.r3.at[k], send_sem=S.s3s.at[0, 0],
                    recv_sem=S.s3r.at[k], device_id=along(0, q), device_id_type=MESH,
                ).wait_recv()
        for path in range(2):
            total = S.r3[0, path].astype(F32)
            for k in range(1, NZ):
                total = total + S.r3[k, path].astype(F32)
            gw_ref[0, :, path * HALF : (path + 1) * HALF] = total[0:BLOCK]

    copies = send_table(2, *pre_grad(1, mean, scale))
    weight_partial(1)
    halo_copies = conv_grad(1, 2, copies)
    first1 = first_exchange(1)
    take_halo(2, halo_copies, S.cg)
    conv_backward(1)
    copy = push(S.gbuf.at[0, p], S.gbuf.at[0, p], S.xs.at[1], S.xr.at[1], along(0, q))
    keep_small(1)
    S.kga[...] = jnp.zeros(S.kga.shape, F32)
    copy.wait_recv()

    act_grad(0)
    copies = send_table(3, *pre_grad(0, None, None))
    second1 = second_exchange(1, first1)
    weight_partial(0)
    halo_copies = conv_grad(0, 3, copies)
    first0 = first_exchange(0)
    third_exchange(1, second1)
    take_halo(3, halo_copies, S.cg)
    conv_backward(0)
    keep_small(0)

    place = x * NY + y
    small = [
        push(
            S.sb.at[lax.rem(x + dx, NX) * NY + lax.rem(y + dy, NY)], S.ar.at[n],
            S.as_.at[n], S.ar_.at[n], plane(dx, dy, p),
        )
        for n, (dx, dy) in enumerate(PLANE[1:])
    ]
    second0 = second_exchange(0, first0)
    for copy in small:
        copy.wait_recv()
    total = S.sb[place]
    for n in range(15):
        total = total + S.ar[n]
    S.zb[z] = total
    small = [
        push(S.zb.at[z], S.zb.at[z], S.zs.at[dz - 1], S.zr.at[dz - 1], depth(dz, p))
        for dz in range(1, NZ)
    ]
    third_exchange(0, second0)
    for dz in range(1, NZ):
        from_z = lax.rem(z + NZ - dz, NZ)
        pltpu.make_async_remote_copy(
            src_ref=S.zb.at[from_z], dst_ref=S.zb.at[from_z], send_sem=S.zs.at[dz - 1],
            recv_sem=S.zr.at[dz - 1], device_id=depth(dz, p), device_id_type=MESH,
        ).wait_recv()
    total = S.zb[0]
    for k in range(1, NZ):
        total = total + S.zb[k]
    S.fs[0] = total[0:16]
    S.fs[1] = total[16:32]
    S.fin[p, place] = S.fs[p]
    small = [
        push(S.fs.at[core[rel]], S.fin.at[p, place], S.gs.at[n], S.gr.at[n], plane(dx, dy, core[rel]))
        for n, (dx, dy, rel) in enumerate(GATHER)
    ]
    finish_third()
    for copy in small:
        copy.wait_recv()
    for h in range(2):
        for c in range(TILES):
            at = slice(h * HALF + c * LANE, h * HALF + (c + 1) * LANE)
            for k in range(4):
                t = c * 5 + k
                gk_ref[0, 8 * k : 8 * k + 8, at] = S.fin[h, t // 2, (t % 2) * 8 : (t % 2) * 8 + 8, :]
            t = c * 5 + 4
            gg_ref[:, at] = S.fin[h, t // 2, (t % 2) * 8 : (t % 2) * 8 + 1, :]
            gb_ref[:, at] = S.fin[h, t // 2, (t % 2) * 8 + 1 : (t % 2) * 8 + 2, :]
    for copy in sends:
        copy.wait_send()


def body(*args):
    shapes = scratch()
    names = list(shapes)
    vmem, hbm = pl.BlockSpec(memory_space=pltpu.VMEM), pl.BlockSpec(memory_space=pl.ANY)

    def kern(*refs):
        main_kernel(names, *refs)

    return pl.pallas_call(
        kern,
        out_shape=(
            jax.ShapeDtypeStruct((1, ROWS, HALF), BF16),
            jax.ShapeDtypeStruct((1, BLOCK, D), F32),
            jax.ShapeDtypeStruct((1, TAPS, D), F32),
            jax.ShapeDtypeStruct((1, D), F32),
            jax.ShapeDtypeStruct((1, D), F32),
        ),
        in_specs=[hbm, hbm, vmem, hbm, vmem, vmem, vmem],
        out_specs=[vmem] * 5,
        scratch_shapes=list(shapes.values()),
        compiler_params=pltpu.CompilerParams(
            collective_id=0, has_side_effects=True, vmem_limit_bytes=56 << 20
        ),
    )(*args)


def solution(mesh):
    return jax.shard_map(
        body,
        mesh=mesh,
        in_specs=(
            P("dp", "seq", None),
            P("dp", "seq", None),
            P("dp", None),
            P("pipe", None, None),
            P("pipe", None, None),
            P("pipe", None),
            P("pipe", None),
        ),
        out_specs=(
            P("dp", "seq", "pipe"),
            P("pipe", ("seq", "dp"), None),
            P("pipe", None, None),
            P("pipe", None),
            P("pipe", None),
        ),
        check_vma=False,
    )
```

```python
import types

import jax
import jax.numpy as jnp
from jax import lax
from jax.experimental import pallas as pl
from jax.experimental.pallas import tpu as pltpu
from jax.sharding import PartitionSpec as P

EPSILON = 1e-05
MESH = pl.DeviceIdType.MESH
F32, BF16 = jnp.float32, jnp.bfloat16
D, HALF, ROWS, TAPS, RIM, UTTS = 1536, 768, 256, 32, 16, 32
LANE, TILES = 128, 6
NX, NY, NZ = 4, 4, 8
SEQ = NX * NZ
BLOCK = 12
STEP, GROUP = 32, 3
PADDED = ROWS + 2 * RIM

PLANE = [(dx, dy) for dx in range(NX) for dy in range(NY)]
OFFSETS = [(s, rel) for s in (-2, -1, 0, 1, 2) for rel in (0, 1) if (s, rel) != (0, 0)]
GATHER = [(dx, dy, rel) for dx, dy in PLANE for rel in (0, 1) if (dx, dy, rel) != (0, 0, 0)]


def scratch():
    vm, dma = pltpu.VMEM, pltpu.SemaphoreType.DMA
    return dict(
        hb=vm((ROWS, HALF), BF16),
        gbuf=vm((2, 2, ROWS, HALF), BF16),
        w=vm((2, HALF, D), BF16),
        pst=vm((2, TILES, 40, LANE), F32),
        pb=vm((2, TILES, 40, LANE), F32),
        seg=vm((PADDED, LANE), F32),
        cnt=vm((8, LANE), F32),
        perm=vm((2, HALF, HALF), BF16),
        xf=vm((2, TILES, PADDED, LANE), F32),
        y=vm((2, TILES, ROWS, LANE), F32),
        inv=vm((2, ROWS, LANE), F32),
        act=vm((2, ROWS, HALF), BF16),
        ag=vm((ROWS, HALF), F32),
        cg=vm((TILES, PADDED, LANE), F32),
        kga=vm((2, TILES, TAPS, 8, LANE), F32),
        gba=vm((2, 2, TILES, 8, LANE), F32),
        halo=vm((4, 2, RIM, HALF), BF16),
        edge=vm((2, 2, RIM, HALF), BF16),
        hx=vm((2, ROWS, HALF), BF16),
        h1=vm((ROWS, HALF), BF16),
        tab=vm((4, 8, LANE), F32),
        tabr=vm((4, 9, 8, LANE), F32),
        gwb=vm((2, 2, HALF, HALF), BF16),
        r1=vm((2, 2, 3, HALF // 4, HALF), BF16),
        s2=vm((2, 2, HALF // 4, HALF), BF16),
        r2=vm((2, 2, 3, HALF // 16, HALF), BF16),
        t3=vm((HALF // 16 + 8, HALF), F32),
        s3=vm((2, 4, 2, 16, HALF), BF16),
        r3=vm((NZ, 2, 16, HALF), BF16),
        sb=vm((16, 32, LANE), F32),
        ar=vm((15, 32, LANE), F32),
        zb=vm((NZ, 32, LANE), F32),
        fs=vm((2, 16, LANE), F32),
        fin=vm((2, 16, 16, LANE), F32),
        lsem=dma((4,)),
        hs=dma((4, 2)), hr=dma((4, 2)),
        ws=dma((2,)), wr=dma((2,)),
        xs=dma((2,)), xr=dma((2,)),
        ts=dma((4, 9)), tr=dma((4, 9)),
        s1s=dma((2, 2, 3)), s1r=dma((2, 2, 3)),
        s2s=dma((2, 2, 3)), s2r=dma((2, 2, 3)),
        s3s=dma((2, 4)), s3r=dma((NZ,)),
        as_=dma((15,)), ar_=dma((15,)),
        zs=dma((7,)), zr=dma((7,)),
        gs=dma((31,)), gr=dma((31,)),
    )


def fold(v):
    total = v[0:8]
    for r in range(8, v.shape[0], 8):
        total = total + v[r : r + 8]
    return total


def dot(a, b):
    return jnp.dot(a, b, preferred_element_type=F32)


def dot_t(a, b):
    return lax.dot_general(a, b, (((1,), (1,)), ((), ())), preferred_element_type=F32)


def cols(c):
    return slice(c * LANE, (c + 1) * LANE)


def main_kernel(names, hid, up, len_ref, w_hbm, ker_ref, gain_ref, bias_ref,
                gi_ref, gw_ref, gk_ref, gg_ref, gb_ref, *refs):
    S = types.SimpleNamespace(**dict(zip(names, refs)))
    i, p, y = lax.axis_index("seq"), lax.axis_index("pipe"), lax.axis_index("dp")
    q = 1 - p
    z, x = lax.div(i, NX), lax.rem(i, NX)
    own_col = pl.multiple_of(p * HALF, HALF)
    oth_col = pl.multiple_of(q * HALF, HALF)

    def dev(seq, pipe, dp):
        return {"seq": seq, "pipe": pipe, "dp": dp}

    def along(offset, pipe):
        return dev(lax.rem(i + offset + SEQ, SEQ), pipe, y)

    def plane(dx, dy, pipe):
        return dev(z * NX + lax.rem(x + dx, NX), pipe, lax.rem(y + dy, NY))

    def depth(dz, pipe):
        return dev(lax.rem(z + dz, NZ) * NX + x, pipe, y)

    core = (p, q)
    sends = []

    def push(src, dst, ssem, rsem, target):
        copy = pltpu.make_async_remote_copy(
            src_ref=src, dst_ref=dst, send_sem=ssem, recv_sem=rsem,
            device_id=target, device_id_type=MESH,
        )
        copy.start()
        sends.append(copy)
        return copy

    loc = [
        pltpu.make_async_copy(hid.at[0, :, pl.ds(own_col, HALF)], S.hb, S.lsem.at[0]),
        pltpu.make_async_copy(w_hbm.at[0, pl.ds(own_col, HALF), :], S.w.at[p], S.lsem.at[1]),
        pltpu.make_async_copy(up.at[0, :, pl.ds(0, HALF)], S.gbuf.at[1, 0], S.lsem.at[2]),
        pltpu.make_async_copy(up.at[0, :, pl.ds(HALF, HALF)], S.gbuf.at[1, 1], S.lsem.at[3]),
    ]
    for copy in loc:
        copy.start()

    barrier = pltpu.get_barrier_semaphore()
    partners = [along(s, core[rel]) for s, rel in OFFSETS]
    partners += [plane(dx, dy, c) for dx, dy in PLANE if (dx, dy) != (0, 0) for c in core]
    partners += [depth(dz, c) for dz in range(1, NZ) for c in core]
    for target in partners:
        pl.semaphore_signal(barrier, inc=1, device_id=target, device_id_type=MESH)

    for h in range(2):
        for c in range(TILES):
            at = slice(h * HALF + c * LANE, h * HALF + (c + 1) * LANE)
            S.pst[h, c, 0:TAPS, :] = ker_ref[0, :, at]
            row = lax.broadcasted_iota(jnp.int32, (8, LANE), 0)
            S.pst[h, c, TAPS:40, :] = jnp.where(
                row == 0, gain_ref[:, at], jnp.where(row == 1, bias_ref[:, at], 0.0)
            )
    for c in range(TILES):
        S.pb[p, c] = S.pst[p, c]

    lens = len_ref[...].astype(F32)
    io0 = lax.broadcasted_iota(jnp.int32, (UTTS, UTTS), 0)
    io1 = lax.broadcasted_iota(jnp.int32, (UTTS, UTTS), 1)
    lens_col = jnp.sum(jnp.where(io0 == io1, lens, 0.0), axis=1, keepdims=True)
    starts = jnp.sum(jnp.where(io0 < io1, lens_col, 0.0), axis=0, keepdims=True)
    bin_total = jnp.sum(lens, axis=1, keepdims=True)
    frame = (lax.broadcasted_iota(jnp.int32, (PADDED, UTTS), 0) + (i * ROWS - RIM)).astype(F32)
    owner = jnp.sum(jnp.where(starts <= frame, 1.0, 0.0), axis=1, keepdims=True) - 1.0
    inside = (frame[:, 0:1] >= 0.0) & (frame[:, 0:1] < bin_total)
    S.seg[...] = jnp.broadcast_to(jnp.where(inside, owner, -2.0), (PADDED, LANE))
    S.cnt[...] = jnp.full((8, LANE), float(D), F32)
    S.cnt[0:1, 0:UTTS] = lens * float(D)

    r = lax.broadcasted_iota(jnp.int32, (HALF, LANE), 0).astype(F32)
    blk = jnp.floor((r + 0.5) / BLOCK)
    word = r - BLOCK * blk
    b4 = jnp.floor((blk + 0.5) / 4.0)
    dig0 = blk - 4.0 * b4
    dig2 = jnp.floor((b4 + 0.5) / 4.0)
    dig1 = b4 - 4.0 * dig2
    lane = lax.broadcasted_iota(jnp.int32, (HALF, LANE), 1).astype(F32)
    for path, (yy, xx) in enumerate(((dig2, dig1), (dig1, dig2))):
        nat = ((dig0 * 4.0 + xx) * 4.0 + yy) * BLOCK + word
        for c in range(TILES):
            S.perm[path, :, cols(c)] = jnp.where(nat == lane + float(c * LANE), 1.0, 0.0).astype(BF16)

    S.kga[...] = jnp.zeros(S.kga.shape, F32)
    S.sb[15] = jnp.zeros((32, LANE), F32)
    S.t3[HALF // 16 :, :] = jnp.zeros((8, HALF), F32)

    pl.semaphore_wait(barrier, len(partners))

    def send_halo(rnd, first, last):
        return [
            push(last, S.halo.at[rnd, 0], S.hs.at[rnd, 0], S.hr.at[rnd, 0], along(1, p)),
            push(first, S.halo.at[rnd, 1], S.hs.at[rnd, 1], S.hr.at[rnd, 1], along(-1, p)),
        ]

    def take_halo(rnd, copies, dst):
        for copy in copies:
            copy.wait_recv()
        for c in range(TILES):
            dst[c, 0:RIM, :] = S.halo[rnd, 0, :, cols(c)].astype(F32)
            dst[c, RIM + ROWS :, :] = S.halo[rnd, 1, :, cols(c)].astype(F32)

    halo_copies = send_halo(
        0,
        hid.at[0, pl.ds(0, RIM), pl.ds(own_col, HALF)],
        hid.at[0, pl.ds(ROWS - RIM, RIM), pl.ds(own_col, HALF)],
    )
    par_copy = push(S.pst.at[q], S.pb.at[p], S.ws.at[0], S.wr.at[0], along(0, q))
    w_copy = push(
        w_hbm.at[0, pl.ds(oth_col, HALF), :], S.w.at[p], S.ws.at[1], S.wr.at[1], along(0, q)
    )

    loc[0].wait()
    for c in range(TILES):
        S.xf[0, c, RIM : RIM + ROWS, :] = S.hb[:, cols(c)].astype(F32)

    steps = ROWS // STEP
    lane_id = lax.broadcasted_iota(jnp.int32, (STEP, LANE), 1).astype(F32)

    def base_of(b):
        return pl.multiple_of(b * STEP, STEP)

    def member(base):
        return S.seg[pl.ds(base + RIM, STEP), :] == lane_id

    def table_add(onehot, v):
        return fold(jnp.where(onehot, jnp.sum(v, axis=1, keepdims=True), 0.0))

    def pick(onehot, row):
        return jnp.sum(jnp.where(onehot, row, 0.0), axis=1, keepdims=True)

    zero_tab = jnp.zeros((8, LANE), F32)

    def send_table(rnd, t1, t2):
        row = lax.broadcasted_iota(jnp.int32, (8, LANE), 0)
        t1 = jnp.sum(t1, axis=0, keepdims=True)
        t2 = jnp.sum(t2, axis=0, keepdims=True)
        S.tab[rnd] = jnp.where(row == 0, t1, jnp.where(row == 1, t2, 0.0))
        return [
            push(S.tab.at[rnd], S.tabr.at[rnd, n], S.ts.at[rnd, n], S.tr.at[rnd, n], along(s, core[rel]))
            for n, (s, rel) in enumerate(OFFSETS)
        ]

    def take_table(rnd, copies):
        total = S.tab[rnd]
        for copy in copies:
            copy.wait_recv()
        for n in range(9):
            total = total + S.tabr[rnd, n]
        count = S.cnt[0:1, :]
        return total[0:1] / count, total[1:2] / count

    def inside_first(step, carry, then):
        carry = lax.fori_loop(1, steps - 1, step, carry)
        then()
        return lax.fori_loop(0, 2, lambda b, held: step(b * (steps - 1), held), carry)

    def conv_forward(s, copies):
        def step(b, carry):
            t1, t2 = carry
            base = base_of(b)
            centre = S.seg[pl.ds(base + RIM, STEP), :]
            first = second = jnp.zeros((STEP, LANE), F32)
            for g in range(0, TILES, GROUP):
                acc = [jnp.zeros((STEP, LANE), F32) for _ in range(GROUP)]
                for j in range(TAPS):
                    same = S.seg[pl.ds(base + j + 1, STEP), :] == centre
                    for c in range(GROUP):
                        window = S.xf[s, g + c, pl.ds(base + j + 1, STEP), :]
                        acc[c] = acc[c] + jnp.where(same, window * S.pb[s, g + c, j : j + 1, :], 0.0)
                for c in range(GROUP):
                    S.y[s, g + c, pl.ds(base, STEP), :] = acc[c]
                    first = first + acc[c]
                    second = second + acc[c] * acc[c]
            onehot = member(base)
            return t1 + table_add(onehot, first), t2 + table_add(onehot, second)

        return inside_first(step, (zero_tab, zero_tab), lambda: take_halo(s, copies, S.xf.at[s]))

    def moments(rnd, copies):
        mean, square = take_table(rnd, copies)
        spread = jnp.maximum(square - mean * mean, 0.0)
        return mean, lax.rsqrt(spread + EPSILON)

    def normalize(s, base, onehot, mean, scale):
        m, v = pick(onehot, mean), pick(onehot, scale)
        S.inv[s, pl.ds(base, STEP), :] = jnp.broadcast_to(v, (STEP, LANE))
        return m, v

    def activate(s, base, c, normed):
        gain, bias = S.pb[s, c, TAPS : TAPS + 1, :], S.pb[s, c, TAPS + 1 : TAPS + 2, :]
        pre = normed * gain + bias
        sig = jax.nn.sigmoid(pre)
        return gain, pre, sig

    par_copy.wait_recv()
    copies = send_table(0, *conv_forward(0, halo_copies))
    mean, scale = moments(0, copies)

    def norm_step(b, _):
        base = base_of(b)
        m, v = normalize(0, base, member(base), mean, scale)
        for c in range(TILES):
            normed = (S.y[0, c, pl.ds(base, STEP), :] - m) * v
            S.y[0, c, pl.ds(base, STEP), :] = normed
            _, pre, sig = activate(0, base, c, normed)
            S.act[0, pl.ds(base, STEP), cols(c)] = (pre * sig).astype(BF16)
        return 0

    lax.fori_loop(0, steps, norm_step, 0)
    loc[1].wait()
    w_copy.wait_recv()
    S.hx[0] = dot(S.act[0], S.w[0, :, pl.ds(oth_col, HALF)]).astype(BF16)
    copy = push(S.hx.at[0], S.hx.at[1], S.xs.at[0], S.xr.at[0], along(0, q))
    S.ag[...] = dot(S.act[0], S.w[0, :, pl.ds(own_col, HALF)])
    copy.wait_recv()

    def out_step(b, _):
        base = base_of(b)
        at = pl.ds(base, STEP)
        S.h1[at, :] = (S.hb[at, :].astype(F32) + (S.ag[at, :] + S.hx[1, at, :].astype(F32))).astype(BF16)
        return 0

    lax.fori_loop(0, steps, out_step, 0)
    halo_copies = send_halo(1, S.h1.at[pl.ds(0, RIM), :], S.h1.at[pl.ds(ROWS - RIM, RIM), :])
    for c in range(TILES):
        S.xf[1, c, RIM : RIM + ROWS, :] = S.h1[:, cols(c)].astype(F32)

    copies = send_table(1, *conv_forward(1, halo_copies))

    def act_grad(s):
        S.ag[...] = dot_t(S.gbuf[s, 0], S.w[s, :, 0:HALF]) + dot_t(S.gbuf[s, 1], S.w[s, :, HALF:])

    loc[2].wait()
    loc[3].wait()
    act_grad(1)
    mean, scale = moments(1, copies)

    def pre_grad(s, mean, scale):
        def step(b, carry):
            t1, t2, gains, biases = carry
            base = base_of(b)
            onehot = member(base)
            at = pl.ds(base, STEP)
            if s == 1:
                m, v = normalize(1, base, onehot, mean, scale)
            first = second = jnp.zeros((STEP, LANE), F32)
            new_gains, new_biases = [], []
            for c in range(TILES):
                normed = S.y[s, c, at, :]
                if s == 1:
                    normed = (normed - m) * v
                    S.y[1, c, at, :] = normed
                gain, pre, sig = activate(s, base, c, normed)
                if s == 1:
                    S.act[1, at, cols(c)] = (pre * sig).astype(BF16)
                grad = S.ag[at, cols(c)] * sig * (1.0 + pre * (1.0 - sig))
                scaled = grad * gain
                S.ag[at, cols(c)] = scaled
                first = first + scaled
                second = second + scaled * normed
                new_gains.append(gains[c] + fold(grad * normed))
                new_biases.append(biases[c] + fold(grad))
            return (t1 + table_add(onehot, first), t2 + table_add(onehot, second),
                    tuple(new_gains), tuple(new_biases))

        zeros = tuple(zero_tab for _ in range(TILES))
        t1, t2, gains, biases = lax.fori_loop(0, steps, step, (zero_tab, zero_tab, zeros, zeros))
        for c in range(TILES):
            S.gba[s, 0, c] = gains[c]
            S.gba[s, 1, c] = biases[c]
        return t1, t2

    def conv_grad(s, rnd, copies):
        mean_a, mean_b = take_table(rnd, copies)

        def step(b, _):
            base = base_of(b)
            onehot = member(base)
            ca, cb = pick(onehot, mean_a), pick(onehot, mean_b)
            at = pl.ds(base, STEP)
            v = S.inv[s, at, :]
            for c in range(TILES):
                S.cg[c, pl.ds(base + RIM, STEP), :] = v * (S.ag[at, cols(c)] - ca - S.y[s, c, at, :] * cb)
            return 0

        lax.fori_loop(0, steps, step, 0)
        for c in range(TILES):
            S.edge[s, 0, :, cols(c)] = S.cg[c, RIM : 2 * RIM, :].astype(BF16)
            S.edge[s, 1, :, cols(c)] = S.cg[c, ROWS : ROWS + RIM, :].astype(BF16)
        return send_halo(rnd, S.edge.at[s, 0], S.edge.at[s, 1])

    def conv_backward(s, then):
        def step(b, _):
            base = base_of(b)
            at = pl.ds(base, STEP)
            centre = S.seg[pl.ds(base + RIM, STEP), :]
            for g in range(0, TILES, GROUP):
                acc = [jnp.zeros((STEP, LANE), F32) for _ in range(GROUP)]
                for j in range(TAPS):
                    same = S.seg[pl.ds(base + TAPS - 1 - j, STEP), :] == centre
                    for c in range(GROUP):
                        window = S.cg[g + c, pl.ds(base + TAPS - 1 - j, STEP), :]
                        acc[c] = acc[c] + jnp.where(same, window * S.pb[s, g + c, j : j + 1, :], 0.0)
                for c in range(GROUP):
                    passed = S.gbuf[s, p, at, cols(g + c)].astype(F32) + acc[c]
                    if s == 1:
                        S.gbuf[0, p, at, cols(g + c)] = passed.astype(BF16)
                    else:
                        gi_ref[0, at, cols(g + c)] = passed.astype(BF16)
            return 0

        inside_first(step, 0, then)

    def kernel_grad(s, low, high):
        def step(b, _):
            base = base_of(b)
            centre = S.seg[pl.ds(base + RIM, STEP), :]
            for g in range(0, TILES, GROUP):
                mine = [S.cg[g + c, pl.ds(base + RIM, STEP), :] for c in range(GROUP)]
                for j in range(TAPS):
                    same = S.seg[pl.ds(base + j + 1, STEP), :] == centre
                    for c in range(GROUP):
                        window = S.xf[s, g + c, pl.ds(base + j + 1, STEP), :]
                        S.kga[s, g + c, j] += fold(jnp.where(same, window * mine[c], 0.0))
            return 0

        lax.fori_loop(low, high, step, 0)

    def keep_small(s):
        row = lax.broadcasted_iota(jnp.int32, (8, LANE), 0)
        for c in range(TILES):
            for k in range(4):
                t = c * 5 + k
                at = slice(s * 16 + (t % 2) * 8, s * 16 + (t % 2) * 8 + 8)
                S.sb[t // 2, at, :] = jnp.sum(S.kga[s, c, 8 * k : 8 * k + 8], axis=1)
            t = c * 5 + 4
            at = slice(s * 16 + (t % 2) * 8, s * 16 + (t % 2) * 8 + 8)
            gsum = jnp.sum(S.gba[s, 0, c], axis=0, keepdims=True)
            bsum = jnp.sum(S.gba[s, 1, c], axis=0, keepdims=True)
            S.sb[t // 2, at, :] = jnp.where(row == 0, gsum, jnp.where(row == 1, bsum, 0.0))

    def weight_partial(s):
        def step(k, _):
            at = pl.ds(pl.multiple_of(k * 256, 256), 256)
            for path in range(2):
                turned = dot_t(S.perm[path, at, :], S.act[s]).astype(BF16)
                S.gwb[s, path, at, :] = dot(turned, S.gbuf[s, path]).astype(BF16)
            return 0

        lax.fori_loop(0, HALF // 256, step, 0)

    def ring_target(path, d):
        return plane(0, d, p) if path == 0 else plane(d, 0, p)

    def ring_index(path, d):
        return lax.rem((y if path == 0 else x) + d, 4)

    q1, q2 = HALF // 4, HALF // 16

    def first_exchange(s):
        return [
            push(
                S.gwb.at[s, path, pl.ds(pl.multiple_of(ring_index(path, d) * q1, q1), q1), :],
                S.r1.at[s, path, d - 1], S.s1s.at[s, path, d - 1], S.s1r.at[s, path, d - 1],
                ring_target(path, d),
            )
            for d in (1, 2, 3) for path in range(2)
        ]

    def second_exchange(s, copies):
        for copy in copies:
            copy.wait_recv()
        for path in range(2):
            def step(k, _):
                at = pl.ds(pl.multiple_of(k * 48, 48), 48)
                mine = pl.ds(pl.multiple_of(ring_index(path, 0) * q1 + k * 48, 48), 48)
                total = S.gwb[s, path, mine, :].astype(F32)
                for d in range(3):
                    total = total + S.r1[s, path, d, at, :].astype(F32)
                S.s2[s, path, at, :] = total.astype(BF16)
                return 0

            lax.fori_loop(0, 4, step, 0)
        return [
            push(
                S.s2.at[s, path, pl.ds(pl.multiple_of(ring_index(1 - path, d) * q2, q2), q2), :],
                S.r2.at[s, path, d - 1], S.s2s.at[s, path, d - 1], S.s2r.at[s, path, d - 1],
                ring_target(1 - path, d),
            )
            for d in (1, 2, 3) for path in range(2)
        ]

    near = lax.div(z, 4) == p

    def third_exchange(s, copies):
        for copy in copies:
            copy.wait_recv()
        for path in range(2):
            mine = pl.ds(pl.multiple_of(ring_index(1 - path, 0) * q2, q2), q2)
            total = S.s2[s, path, mine, :].astype(F32)
            for d in range(3):
                total = total + S.r2[s, path, d].astype(F32)
            S.t3[0:q2, :] = total
            for k in range(4):
                S.s3[s, k, path] = S.t3[BLOCK * k : BLOCK * k + 16, :].astype(BF16)
        for k in range(4):
            target_z = 4 * p + k
            stays = (target_z == z) & (p == s)
            copy = pltpu.make_async_remote_copy(
                src_ref=S.s3.at[s, k], dst_ref=S.r3.at[z], send_sem=S.s3s.at[s, k],
                recv_sem=S.s3r.at[z], device_id=dev(target_z * NX + x, s, y), device_id_type=MESH,
            )

            @pl.when(jnp.logical_not(stays))
            def _():
                copy.start()

            @pl.when(stays)
            def _():
                S.r3[z] = S.s3[s, k]

    def finish_third():
        for s in range(2):
            for k in range(4):
                target_z = 4 * p + k
                stays = (target_z == z) & (p == s)

                @pl.when(jnp.logical_not(stays))
                def _():
                    pltpu.make_async_remote_copy(
                        src_ref=S.s3.at[s, k], dst_ref=S.r3.at[z], send_sem=S.s3s.at[s, k],
                        recv_sem=S.s3r.at[z], device_id=dev(target_z * NX + x, s, y),
                        device_id_type=MESH,
                    ).wait_send()
        for k in range(NZ):
            @pl.when(jnp.logical_not((z == k) & near))
            def _():
                pltpu.make_async_remote_copy(
                    src_ref=S.s3.at[0, 0], dst_ref=S.r3.at[k], send_sem=S.s3s.at[0, 0],
                    recv_sem=S.s3r.at[k], device_id=along(0, q), device_id_type=MESH,
                ).wait_recv()
        for path in range(2):
            total = S.r3[0, path].astype(F32)
            for k in range(1, NZ):
                total = total + S.r3[k, path].astype(F32)
            for k in range(BLOCK):
                gw_ref[k, :, path * HALF : (path + 1) * HALF] = total[k : k + 1]

    copies = send_table(2, *pre_grad(1, mean, scale))
    weight_partial(1)
    halo_copies = conv_grad(1, 2, copies)
    first1 = first_exchange(1)

    def while_away():
        kernel_grad(1, 0, 4)
        take_halo(2, halo_copies, S.cg)

    conv_backward(1, while_away)
    copy = push(S.gbuf.at[0, p], S.gbuf.at[0, p], S.xs.at[1], S.xr.at[1], along(0, q))
    copy.wait_recv()

    act_grad(0)
    copies = send_table(3, *pre_grad(0, None, None))
    weight_partial(0)
    kernel_grad(1, 4, steps)
    keep_small(1)
    second1 = second_exchange(1, first1)
    halo_copies = conv_grad(0, 3, copies)
    first0 = first_exchange(0)
    kernel_grad(0, 0, steps)
    keep_small(0)

    place = x * NY + y
    small = [
        push(
            S.sb.at[lax.rem(x + dx, NX) * NY + lax.rem(y + dy, NY)], S.ar.at[n],
            S.as_.at[n], S.ar_.at[n], plane(dx, dy, p),
        )
        for n, (dx, dy) in enumerate(PLANE[1:])
    ]
    third_exchange(1, second1)
    conv_backward(0, lambda: take_halo(3, halo_copies, S.cg))
    for copy in small:
        copy.wait_recv()
    total = S.sb[place]
    for n in range(15):
        total = total + S.ar[n]
    S.zb[z] = total
    small = [
        push(S.zb.at[z], S.zb.at[z], S.zs.at[dz - 1], S.zr.at[dz - 1], depth(dz, p))
        for dz in range(1, NZ)
    ]
    second0 = second_exchange(0, first0)
    for dz in range(1, NZ):
        from_z = lax.rem(z + NZ - dz, NZ)
        pltpu.make_async_remote_copy(
            src_ref=S.zb.at[from_z], dst_ref=S.zb.at[from_z], send_sem=S.zs.at[dz - 1],
            recv_sem=S.zr.at[dz - 1], device_id=depth(dz, p), device_id_type=MESH,
        ).wait_recv()
    total = S.zb[0]
    for k in range(1, NZ):
        total = total + S.zb[k]
    S.fs[0] = total[0:16]
    S.fs[1] = total[16:32]
    S.fin[p, place] = S.fs[p]
    small = [
        push(S.fs.at[core[rel]], S.fin.at[p, place], S.gs.at[n], S.gr.at[n], plane(dx, dy, core[rel]))
        for n, (dx, dy, rel) in enumerate(GATHER)
    ]
    third_exchange(0, second0)
    finish_third()
    for copy in small:
        copy.wait_recv()
    for h in range(2):
        for c in range(TILES):
            at = slice(h * HALF + c * LANE, h * HALF + (c + 1) * LANE)
            for k in range(4):
                t = c * 5 + k
                gk_ref[0, 8 * k : 8 * k + 8, at] = S.fin[h, t // 2, (t % 2) * 8 : (t % 2) * 8 + 8, :]
            t = c * 5 + 4
            gg_ref[:, at] = S.fin[h, t // 2, (t % 2) * 8 : (t % 2) * 8 + 1, :]
            gb_ref[:, at] = S.fin[h, t // 2, (t % 2) * 8 + 1 : (t % 2) * 8 + 2, :]
    for copy in sends:
        copy.wait_send()


def relay_kernel(*refs):
    for k in range(5):
        refs[5 + k][...] = refs[k][...]


def body(*args):
    shapes = scratch()
    names = list(shapes)
    vmem, hbm = pl.BlockSpec(memory_space=pltpu.VMEM), pl.BlockSpec(memory_space=pl.ANY)

    def kern(*refs):
        main_kernel(names, *refs)

    results = pl.pallas_call(
        kern,
        out_shape=(
            jax.ShapeDtypeStruct((1, ROWS, HALF), BF16),
            jax.ShapeDtypeStruct((BLOCK, 1, D), F32),
            jax.ShapeDtypeStruct((1, TAPS, D), F32),
            jax.ShapeDtypeStruct((1, D), F32),
            jax.ShapeDtypeStruct((1, D), F32),
        ),
        in_specs=[hbm, hbm, vmem, hbm, vmem, vmem, vmem],
        out_specs=[vmem] * 5,
        scratch_shapes=list(shapes.values()),
        compiler_params=pltpu.CompilerParams(
            collective_id=0, has_side_effects=True, vmem_limit_bytes=56 << 20
        ),
    )(*args)
    gi, gw, gk, gg, gb = pl.pallas_call(
        relay_kernel,
        out_shape=tuple(jax.ShapeDtypeStruct(r.shape, r.dtype) for r in results),
        in_specs=[vmem] * 5,
        out_specs=[vmem] * 5,
    )(*results)
    return gi, gw.reshape(1, BLOCK, D), gk, gg, gb


def solution(mesh):
    return jax.shard_map(
        body,
        mesh=mesh,
        in_specs=(
            P("dp", "seq", None),
            P("dp", "seq", None),
            P("dp", None),
            P("pipe", None, None),
            P("pipe", None, None),
            P("pipe", None),
            P("pipe", None),
        ),
        out_specs=(
            P("dp", "seq", "pipe"),
            P("pipe", ("seq", "dp"), None),
            P("pipe", None, None),
            P("pipe", None),
            P("pipe", None),
        ),
        check_vma=False,
    )
```

```python
import types

import jax
import jax.numpy as jnp
from jax import lax
from jax.experimental import pallas as pl
from jax.experimental.pallas import tpu as pltpu
from jax.sharding import PartitionSpec as P

EPSILON = 1e-05
MESH = pl.DeviceIdType.MESH
F32, BF16 = jnp.float32, jnp.bfloat16
D, HALF, ROWS, TAPS, RIM, UTTS = 1536, 768, 256, 32, 16, 32
LANE, TILES = 128, 6
NX, NY, NZ = 4, 4, 8
SEQ = NX * NZ
BLOCK = 12
STEP, GROUP = 32, 3
PADDED = ROWS + 2 * RIM

PLANE = [(dx, dy) for dx in range(NX) for dy in range(NY)]
OFFSETS = [(s, rel) for s in (-2, -1, 0, 1, 2) for rel in (0, 1) if (s, rel) != (0, 0)]
GATHER = [(dx, dy, rel) for dx, dy in PLANE for rel in (0, 1) if (dx, dy, rel) != (0, 0, 0)]


def scratch():
    vm, dma = pltpu.VMEM, pltpu.SemaphoreType.DMA
    return dict(
        hb=vm((ROWS, HALF), BF16),
        gbuf=vm((2, 2, ROWS, HALF), BF16),
        w=vm((2, HALF, D), BF16),
        pst=vm((2, TILES, 40, LANE), F32),
        pb=vm((2, TILES, 40, LANE), F32),
        seg=vm((PADDED, LANE), F32),
        cnt=vm((8, LANE), F32),
        perm=vm((2, HALF, HALF), BF16),
        xf=vm((2, TILES, PADDED, LANE), F32),
        y=vm((2, TILES, PADDED, LANE), F32),
        nrm=vm((2, TILES, ROWS, LANE), F32),
        cb=vm((3, TILES, ROWS, LANE), F32),
        inv=vm((2, ROWS, LANE), F32),
        act=vm((2, ROWS, HALF), BF16),
        ag=vm((2, ROWS, HALF), F32),
        part=vm((ROWS, HALF), F32),
        cg=vm((TILES, PADDED, LANE), F32),
        kga=vm((2, TILES, TAPS, 8, LANE), F32),
        gba=vm((2, 2, TILES, 8, LANE), F32),
        halo=vm((5, 2, RIM, HALF), BF16),
        edge=vm((3, 2, RIM, HALF), BF16),
        hx=vm((2, ROWS, HALF), BF16),
        h1=vm((ROWS, HALF), BF16),
        tab=vm((4, 8, LANE), F32),
        tabr=vm((4, 9, 8, LANE), F32),
        turn=vm((2, 2, HALF, ROWS), BF16),
        ta=vm((2, 4, 2, HALF // 4, ROWS), BF16),
        gq=vm((2, 3, ROWS, HALF), BF16),
        s2=vm((2, 2, HALF // 4, HALF), BF16),
        r2=vm((2, 3, 2, HALF // 16, HALF), BF16),
        t3=vm((HALF // 16 + 8, HALF), F32),
        s3=vm((2, NZ, 16, HALF), BF16),
        r3=vm((NZ, 2, 16, HALF), BF16),
        sb=vm((16, 32, LANE), F32),
        ar=vm((15, 32, LANE), F32),
        zb=vm((NZ, 32, LANE), F32),
        fs=vm((2, 16, LANE), F32),
        fin=vm((2, 16, 16, LANE), F32),
        lsem=dma((4,)),
        hs=dma((5, 2)), hr=dma((5, 2)),
        ws=dma((2,)), wr=dma((2,)),
        xs=dma((2,)), xr=dma((2,)),
        ts=dma((4, 9)), tr=dma((4, 9)),
        tas=dma((2, 4, 2)), tar=dma((2, 4, 2)),
        gqs=dma((2, 3)), gqr=dma((2, 3)),
        s2s=dma((2, 3)), s2r=dma((2, 3)),
        s3s=dma((2, NZ)), s3r=dma((NZ, 2)),
        as_=dma((15,)), ar_=dma((15,)),
        zs=dma((7,)), zr=dma((7,)),
        gs=dma((31,)), gr=dma((31,)),
    )


def fold(v):
    total = v[0:8]
    for r in range(8, v.shape[0], 8):
        total = total + v[r : r + 8]
    return total


def dot(a, b):
    return jnp.dot(a, b, preferred_element_type=F32)


def dot_t(a, b):
    return lax.dot_general(a, b, (((1,), (1,)), ((), ())), preferred_element_type=F32)


def cols(c):
    return slice(c * LANE, (c + 1) * LANE)


def main_kernel(names, hid, up, len_ref, w_hbm, ker_ref, gain_ref, bias_ref,
                gi_ref, gw_ref, gk_ref, gg_ref, gb_ref, *refs):
    S = types.SimpleNamespace(**dict(zip(names, refs)))
    i, p, y = lax.axis_index("seq"), lax.axis_index("pipe"), lax.axis_index("dp")
    q = 1 - p
    z, x = lax.div(i, NX), lax.rem(i, NX)
    own_col = pl.multiple_of(p * HALF, HALF)
    oth_col = pl.multiple_of(q * HALF, HALF)

    def dev(seq, pipe, dp):
        return {"seq": seq, "pipe": pipe, "dp": dp}

    def along(offset, pipe):
        return dev(lax.rem(i + offset + SEQ, SEQ), pipe, y)

    def plane(dx, dy, pipe):
        return dev(z * NX + lax.rem(x + dx, NX), pipe, lax.rem(y + dy, NY))

    def depth(dz, pipe):
        return dev(lax.rem(z + dz, NZ) * NX + x, pipe, y)

    core = (p, q)
    sends = []

    def push(src, dst, ssem, rsem, target):
        copy = pltpu.make_async_remote_copy(
            src_ref=src, dst_ref=dst, send_sem=ssem, recv_sem=rsem,
            device_id=target, device_id_type=MESH,
        )
        copy.start()
        sends.append(copy)
        return copy

    loc = [
        pltpu.make_async_copy(hid.at[0, :, pl.ds(own_col, HALF)], S.hb, S.lsem.at[0]),
        pltpu.make_async_copy(w_hbm.at[0, pl.ds(own_col, HALF), :], S.w.at[p], S.lsem.at[1]),
        pltpu.make_async_copy(up.at[0, :, pl.ds(0, HALF)], S.gbuf.at[1, 0], S.lsem.at[2]),
        pltpu.make_async_copy(up.at[0, :, pl.ds(HALF, HALF)], S.gbuf.at[1, 1], S.lsem.at[3]),
    ]
    for copy in loc:
        copy.start()

    barrier = pltpu.get_barrier_semaphore()
    partners = [along(s, core[rel]) for s, rel in OFFSETS]
    partners += [plane(dx, dy, c) for dx, dy in PLANE if (dx, dy) != (0, 0) for c in core]
    partners += [depth(dz, c) for dz in range(1, NZ) for c in core]
    for target in partners:
        pl.semaphore_signal(barrier, inc=1, device_id=target, device_id_type=MESH)

    for h in range(2):
        for c in range(TILES):
            at = slice(h * HALF + c * LANE, h * HALF + (c + 1) * LANE)
            S.pst[h, c, 0:TAPS, :] = ker_ref[0, :, at]
            row = lax.broadcasted_iota(jnp.int32, (8, LANE), 0)
            S.pst[h, c, TAPS:40, :] = jnp.where(
                row == 0, gain_ref[:, at], jnp.where(row == 1, bias_ref[:, at], 0.0)
            )
    for c in range(TILES):
        S.pb[p, c] = S.pst[p, c]

    lens = len_ref[...].astype(F32)
    io0 = lax.broadcasted_iota(jnp.int32, (UTTS, UTTS), 0)
    io1 = lax.broadcasted_iota(jnp.int32, (UTTS, UTTS), 1)
    lens_col = jnp.sum(jnp.where(io0 == io1, lens, 0.0), axis=1, keepdims=True)
    starts = jnp.sum(jnp.where(io0 < io1, lens_col, 0.0), axis=0, keepdims=True)
    bin_total = jnp.sum(lens, axis=1, keepdims=True)
    frame = (lax.broadcasted_iota(jnp.int32, (PADDED, UTTS), 0) + (i * ROWS - RIM)).astype(F32)
    owner = jnp.sum(jnp.where(starts <= frame, 1.0, 0.0), axis=1, keepdims=True) - 1.0
    inside = (frame[:, 0:1] >= 0.0) & (frame[:, 0:1] < bin_total)
    S.seg[...] = jnp.broadcast_to(jnp.where(inside, owner, -2.0), (PADDED, LANE))
    S.cnt[...] = jnp.full((8, LANE), float(D), F32)
    S.cnt[0:1, 0:UTTS] = lens * float(D)

    r = lax.broadcasted_iota(jnp.int32, (HALF, LANE), 0).astype(F32)
    blk = jnp.floor((r + 0.5) / BLOCK)
    word = r - BLOCK * blk
    b4 = jnp.floor((blk + 0.5) / 4.0)
    dig0 = blk - 4.0 * b4
    dig2 = jnp.floor((b4 + 0.5) / 4.0)
    dig1 = b4 - 4.0 * dig2
    lane = lax.broadcasted_iota(jnp.int32, (HALF, LANE), 1).astype(F32)
    for path, (yy, xx) in enumerate(((dig2, dig1), (dig1, dig2))):
        nat = ((dig0 * 4.0 + xx) * 4.0 + yy) * BLOCK + word
        for c in range(TILES):
            S.perm[path, :, cols(c)] = jnp.where(nat == lane + float(c * LANE), 1.0, 0.0).astype(BF16)

    S.kga[...] = jnp.zeros(S.kga.shape, F32)
    S.sb[15] = jnp.zeros((32, LANE), F32)
    S.t3[HALF // 16 :, :] = jnp.zeros((8, HALF), F32)

    pl.semaphore_wait(barrier, len(partners))

    def send_halo(rnd, first, last):
        return [
            push(last, S.halo.at[rnd, 0], S.hs.at[rnd, 0], S.hr.at[rnd, 0], along(1, p)),
            push(first, S.halo.at[rnd, 1], S.hs.at[rnd, 1], S.hr.at[rnd, 1], along(-1, p)),
        ]

    def take_halo(rnd, copies, dst):
        for copy in copies:
            copy.wait_recv()
        for c in range(TILES):
            dst[c, 0:RIM, :] = S.halo[rnd, 0, :, cols(c)].astype(F32)
            dst[c, RIM + ROWS :, :] = S.halo[rnd, 1, :, cols(c)].astype(F32)

    halo_copies = send_halo(
        0,
        hid.at[0, pl.ds(0, RIM), pl.ds(own_col, HALF)],
        hid.at[0, pl.ds(ROWS - RIM, RIM), pl.ds(own_col, HALF)],
    )
    par_copy = push(S.pst.at[q], S.pb.at[p], S.ws.at[0], S.wr.at[0], along(0, q))
    w_copy = push(
        w_hbm.at[0, pl.ds(oth_col, HALF), :], S.w.at[p], S.ws.at[1], S.wr.at[1], along(0, q)
    )

    loc[0].wait()
    for c in range(TILES):
        S.xf[0, c, RIM : RIM + ROWS, :] = S.hb[:, cols(c)].astype(F32)

    steps = ROWS // STEP
    lane_id = lax.broadcasted_iota(jnp.int32, (STEP, LANE), 1).astype(F32)

    def base_of(b):
        return pl.multiple_of(b * STEP, STEP)

    def member(base):
        return S.seg[pl.ds(base + RIM, STEP), :] == lane_id

    def table_add(onehot, v):
        return fold(jnp.where(onehot, jnp.sum(v, axis=1, keepdims=True), 0.0))

    def pick(onehot, row):
        return jnp.sum(jnp.where(onehot, row, 0.0), axis=1, keepdims=True)

    zero_tab = jnp.zeros((8, LANE), F32)

    def send_table(rnd, t1, t2):
        row = lax.broadcasted_iota(jnp.int32, (8, LANE), 0)
        t1 = jnp.sum(t1, axis=0, keepdims=True)
        t2 = jnp.sum(t2, axis=0, keepdims=True)
        S.tab[rnd] = jnp.where(row == 0, t1, jnp.where(row == 1, t2, 0.0))
        return [
            push(S.tab.at[rnd], S.tabr.at[rnd, n], S.ts.at[rnd, n], S.tr.at[rnd, n], along(s, core[rel]))
            for n, (s, rel) in enumerate(OFFSETS)
        ]

    def take_table(rnd, copies):
        total = S.tab[rnd]
        for copy in copies:
            copy.wait_recv()
        for n in range(9):
            total = total + S.tabr[rnd, n]
        count = S.cnt[0:1, :]
        return total[0:1] / count, total[1:2] / count

    def inside_first(step, carry, then):
        carry = lax.fori_loop(1, steps - 1, step, carry)
        then()
        return lax.fori_loop(0, 2, lambda b, held: step(b * (steps - 1), held), carry)

    def conv_forward(s, copies):
        def step(b, carry):
            t1, t2 = carry
            base = base_of(b)
            centre = S.seg[pl.ds(base + RIM, STEP), :]
            first = second = jnp.zeros((STEP, LANE), F32)
            for g in range(0, TILES, GROUP):
                acc = [jnp.zeros((STEP, LANE), F32) for _ in range(GROUP)]
                for j in range(TAPS):
                    same = S.seg[pl.ds(base + j + 1, STEP), :] == centre
                    for c in range(GROUP):
                        window = S.xf[s, g + c, pl.ds(base + j + 1, STEP), :]
                        acc[c] = acc[c] + jnp.where(same, window * S.pb[s, g + c, j : j + 1, :], 0.0)
                for c in range(GROUP):
                    S.y[s, g + c, pl.ds(base + RIM, STEP), :] = acc[c]
                    first = first + acc[c]
                    second = second + acc[c] * acc[c]
            onehot = member(base)
            return t1 + table_add(onehot, first), t2 + table_add(onehot, second)

        return inside_first(step, (zero_tab, zero_tab), lambda: take_halo(s, copies, S.xf.at[s]))

    def moments(rnd, copies):
        mean, square = take_table(rnd, copies)
        spread = jnp.maximum(square - mean * mean, 0.0)
        return mean, lax.rsqrt(spread + EPSILON)

    def normalize(s, base, onehot, mean, scale):
        m, v = pick(onehot, mean), pick(onehot, scale)
        S.inv[s, pl.ds(base, STEP), :] = jnp.broadcast_to(v, (STEP, LANE))
        return m, v

    def activate(s, base, c, normed):
        gain, bias = S.pb[s, c, TAPS : TAPS + 1, :], S.pb[s, c, TAPS + 1 : TAPS + 2, :]
        pre = normed * gain + bias
        sig = jax.nn.sigmoid(pre)
        return gain, pre, sig

    def act_grad(s):
        S.ag[s] = dot_t(S.gbuf[s, 0], S.w[s, :, 0:HALF]) + dot_t(S.gbuf[s, 1], S.w[s, :, HALF:])

    def pre_grad(s, mean, scale):
        def step(b, carry):
            t1, t2, gains, biases = carry
            base = base_of(b)
            onehot = member(base)
            at = pl.ds(base, STEP)
            if s == 1:
                m, v = normalize(1, base, onehot, mean, scale)
            first = second = jnp.zeros((STEP, LANE), F32)
            new_gains, new_biases = [], []
            for c in range(TILES):
                if s == 1:
                    normed = (S.y[1, c, pl.ds(base + RIM, STEP), :] - m) * v
                    S.nrm[1, c, at, :] = normed
                else:
                    normed = S.nrm[0, c, at, :]
                gain, pre, sig = activate(s, base, c, normed)
                if s == 1:
                    S.act[1, at, cols(c)] = (pre * sig).astype(BF16)
                grad = S.ag[s, at, cols(c)] * sig * (1.0 + pre * (1.0 - sig))
                scaled = grad * gain
                S.ag[s, at, cols(c)] = scaled
                if s == 1:
                    S.cg[c, pl.ds(base + RIM, STEP), :] = scaled
                first = first + scaled
                second = second + scaled * normed
                new_gains.append(gains[c] + fold(grad * normed))
                new_biases.append(biases[c] + fold(grad))
            return (t1 + table_add(onehot, first), t2 + table_add(onehot, second),
                    tuple(new_gains), tuple(new_biases))

        zeros = tuple(zero_tab for _ in range(TILES))
        t1, t2, gains, biases = lax.fori_loop(0, steps, step, (zero_tab, zero_tab, zeros, zeros))
        for c in range(TILES):
            S.gba[s, 0, c] = gains[c]
            S.gba[s, 1, c] = biases[c]
        return t1, t2

    def conv_grad(s, mean_a, mean_b):
        def step(b, _):
            base = base_of(b)
            onehot = member(base)
            ca, cb = pick(onehot, mean_a), pick(onehot, mean_b)
            at = pl.ds(base, STEP)
            v = S.inv[s, at, :]
            for c in range(TILES):
                S.cg[c, pl.ds(base + RIM, STEP), :] = v * (S.ag[s, at, cols(c)] - ca - S.nrm[s, c, at, :] * cb)
            return 0

        lax.fori_loop(0, steps, step, 0)

    def send_edges(rnd, k, src):
        for c in range(TILES):
            S.edge[k, 0, :, cols(c)] = src[c, RIM : 2 * RIM, :].astype(BF16)
            S.edge[k, 1, :, cols(c)] = src[c, ROWS : ROWS + RIM, :].astype(BF16)
        return send_halo(rnd, S.edge.at[k, 0], S.edge.at[k, 1])

    def back_step(k, src):
        def step(b, _):
            base = base_of(b)
            centre = S.seg[pl.ds(base + RIM, STEP), :]
            for g in range(0, TILES, GROUP):
                acc = [jnp.zeros((STEP, LANE), F32) for _ in range(GROUP)]
                for j in range(TAPS):
                    same = S.seg[pl.ds(base + TAPS - 1 - j, STEP), :] == centre
                    for c in range(GROUP):
                        term = S.pb[1, g + c, j : j + 1, :]
                        if src is not None:
                            term = src[g + c, pl.ds(base + TAPS - 1 - j, STEP), :] * term
                        acc[c] = acc[c] + jnp.where(same, term, 0.0)
                for c in range(GROUP):
                    S.cb[k, g + c, pl.ds(base, STEP), :] = acc[c]
            return 0

        return step

    def back_inner(k, src):
        lax.fori_loop(1, steps - 1, back_step(k, src), 0)

    def back_outer(k, src):
        lax.fori_loop(0, 2, lambda b, _: back_step(k, src)(b * (steps - 1), 0), 0)

    def pass_down(mean, mean_a, mean_b):
        def step(b, _):
            base = base_of(b)
            onehot = member(base)
            at = pl.ds(base, STEP)
            v = S.inv[1, at, :]
            slope = pick(onehot, mean_b) * v
            level = pick(onehot, mean_a) - slope * pick(onehot, mean)
            for c in range(TILES):
                back = v * (S.cb[2, c, at, :] - level * S.cb[0, c, at, :] - slope * S.cb[1, c, at, :])
                S.gbuf[0, p, at, cols(c)] = (S.gbuf[1, p, at, cols(c)].astype(F32) + back).astype(BF16)
            return 0

        lax.fori_loop(0, steps, step, 0)

    def conv_backward(s, then):
        def step(b, _):
            base = base_of(b)
            at = pl.ds(base, STEP)
            centre = S.seg[pl.ds(base + RIM, STEP), :]
            for g in range(0, TILES, GROUP):
                acc = [jnp.zeros((STEP, LANE), F32) for _ in range(GROUP)]
                for j in range(TAPS):
                    same = S.seg[pl.ds(base + TAPS - 1 - j, STEP), :] == centre
                    for c in range(GROUP):
                        window = S.cg[g + c, pl.ds(base + TAPS - 1 - j, STEP), :]
                        acc[c] = acc[c] + jnp.where(same, window * S.pb[s, g + c, j : j + 1, :], 0.0)
                for c in range(GROUP):
                    passed = S.gbuf[s, p, at, cols(g + c)].astype(F32) + acc[c]
                    gi_ref[0, at, cols(g + c)] = passed.astype(BF16)
            return 0

        inside_first(step, 0, then)

    def kernel_grad(s, low, high):
        def step(b, _):
            base = base_of(b)
            centre = S.seg[pl.ds(base + RIM, STEP), :]
            for g in range(0, TILES, GROUP):
                mine = [S.cg[g + c, pl.ds(base + RIM, STEP), :] for c in range(GROUP)]
                for j in range(TAPS):
                    same = S.seg[pl.ds(base + j + 1, STEP), :] == centre
                    for c in range(GROUP):
                        window = S.xf[s, g + c, pl.ds(base + j + 1, STEP), :]
                        S.kga[s, g + c, j] += fold(jnp.where(same, window * mine[c], 0.0))
            return 0

        lax.fori_loop(low, high, step, 0)

    def keep_small(s):
        row = lax.broadcasted_iota(jnp.int32, (8, LANE), 0)
        for c in range(TILES):
            for k in range(4):
                t = c * 5 + k
                at = slice(s * 16 + (t % 2) * 8, s * 16 + (t % 2) * 8 + 8)
                S.sb[t // 2, at, :] = jnp.sum(S.kga[s, c, 8 * k : 8 * k + 8], axis=1)
            t = c * 5 + 4
            at = slice(s * 16 + (t % 2) * 8, s * 16 + (t % 2) * 8 + 8)
            gsum = jnp.sum(S.gba[s, 0, c], axis=0, keepdims=True)
            bsum = jnp.sum(S.gba[s, 1, c], axis=0, keepdims=True)
            S.sb[t // 2, at, :] = jnp.where(row == 0, gsum, jnp.where(row == 1, bsum, 0.0))

    q1, q2 = HALF // 4, HALF // 16
    first_place = jnp.where(p == 0, y, x)
    second_place = jnp.where(p == 0, x, y)

    def first_ring(d, path):
        return plane(d * path, d * (1 - path), path)

    def second_ring(d):
        return plane(d * (1 - p), d * p, p)

    def send_cotangent(s):
        return [
            push(S.gbuf.at[s, p], S.gq.at[s, d - 1], S.gqs.at[s, d - 1], S.gqr.at[s, d - 1], first_ring(d, p))
            for d in (1, 3, 2)
        ]

    def turn_activation(s):
        def step(k, _):
            at = pl.ds(pl.multiple_of(k * 256, 256), 256)
            for path in range(2):
                S.turn[s, path, at, :] = dot_t(S.perm[path, at, :], S.act[s]).astype(BF16)
            return 0

        lax.fori_loop(0, HALF // 256, step, 0)

    def push_activation(s):
        copies = []
        for d in range(4):
            for rel in range(2):
                path = core[rel]
                place = lax.rem(jnp.where(path == 0, y, x) + d, 4)
                rows = pl.ds(pl.multiple_of(place * q1, q1), q1)
                if (d, rel) == (0, 0):
                    S.ta[s, 0, p] = S.turn[s, p, rows, :]
                else:
                    copies.append(push(
                        S.turn.at[s, path, rows, :], S.ta.at[s, d, p], S.tas.at[s, d, rel], S.tar.at[s, d, rel],
                        first_ring(d, path),
                    ))
        return copies

    def first_sum(s, copies):
        for copy in copies:
            copy.wait_recv()
        for h in range(2):
            total = dot(S.ta[s, 0, h], S.gbuf[s, p])
            for d in range(3):
                total = total + dot(S.ta[s, d + 1, h], S.gq[s, d])
            S.s2[s, h] = total.astype(BF16)
        return [
            push(
                S.s2.at[s, :, pl.ds(pl.multiple_of(lax.rem(second_place + d, 4) * q2, q2), q2), :],
                S.r2.at[s, d - 1], S.s2s.at[s, d - 1], S.s2r.at[s, d - 1], second_ring(d),
            )
            for d in (1, 3, 2)
        ]

    def third_copy(s, dz):
        rel = jnp.where(p == s, 0, 1)
        return pltpu.make_async_remote_copy(
            src_ref=S.s3.at[s, lax.rem(z + dz, NZ)], dst_ref=S.r3.at[dz, rel], send_sem=S.s3s.at[s, dz],
            recv_sem=S.s3r.at[dz, rel], device_id=depth(dz, s), device_id_type=MESH,
        )

    def second_sum(s, copies):
        for copy in copies:
            copy.wait_recv()
        mine = pl.ds(pl.multiple_of(second_place * q2, q2), q2)
        for h in range(2):
            total = S.s2[s, h, mine, :].astype(F32)
            for d in range(3):
                total = total + S.r2[s, d, h].astype(F32)
            S.t3[0:q2, :] = total
            for k in range(4):
                S.s3[s, 4 * h + k] = S.t3[BLOCK * k : BLOCK * k + 16, :].astype(BF16)
        for dz in range(1, NZ):
            third_copy(s, dz).start()

        @pl.when(p != s)
        def _():
            third_copy(s, 0).start()

        @pl.when(p == s)
        def _():
            S.r3[0, 0] = S.s3[s, z]

    def third_sum():
        for s in range(2):
            for dz in range(1, NZ):
                third_copy(s, dz).wait_send()

            @pl.when(p != s)
            def _():
                third_copy(s, 0).wait_send()
        for rel, at in ((0, own_col), (1, oth_col)):
            total = jnp.zeros((16, HALF), F32)
            for dz in range(NZ):
                if (dz, rel) != (0, 0):
                    pltpu.make_async_remote_copy(
                        src_ref=S.s3.at[0, 0], dst_ref=S.r3.at[dz, rel], send_sem=S.s3s.at[0, 0],
                        recv_sem=S.s3r.at[dz, rel], device_id=along(0, q), device_id_type=MESH,
                    ).wait_recv()
                total = total + S.r3[dz, rel].astype(F32)
            for k in range(BLOCK):
                gw_ref[k, :, pl.ds(at, HALF)] = total[k : k + 1]

    loc[2].wait()
    loc[3].wait()
    cotangent1 = send_cotangent(1)
    par_copy.wait_recv()
    copies = send_table(0, *conv_forward(0, halo_copies))
    lax.fori_loop(0, steps, back_step(0, None), 0)
    loc[1].wait()
    w_copy.wait_recv()
    act_grad(1)
    mean, scale = moments(0, copies)

    def norm_step(b, _):
        base = base_of(b)
        m, v = normalize(0, base, member(base), mean, scale)
        for c in range(TILES):
            normed = (S.y[0, c, pl.ds(base + RIM, STEP), :] - m) * v
            S.nrm[0, c, pl.ds(base, STEP), :] = normed
            _, pre, sig = activate(0, base, c, normed)
            S.act[0, pl.ds(base, STEP), cols(c)] = (pre * sig).astype(BF16)
        return 0

    lax.fori_loop(0, steps, norm_step, 0)
    S.hx[0] = dot(S.act[0], S.w[0, :, pl.ds(oth_col, HALF)]).astype(BF16)
    copy = push(S.hx.at[0], S.hx.at[1], S.xs.at[0], S.xr.at[0], along(0, q))
    S.part[...] = dot(S.act[0], S.w[0, :, pl.ds(own_col, HALF)])
    turn_activation(0)
    copy.wait_recv()

    def out_step(b, _):
        base = base_of(b)
        at = pl.ds(base, STEP)
        S.h1[at, :] = (S.hb[at, :].astype(F32) + (S.part[at, :] + S.hx[1, at, :].astype(F32))).astype(BF16)
        return 0

    lax.fori_loop(0, steps, out_step, 0)
    halo_copies = send_halo(1, S.h1.at[pl.ds(0, RIM), :], S.h1.at[pl.ds(ROWS - RIM, RIM), :])
    for c in range(TILES):
        S.xf[1, c, RIM : RIM + ROWS, :] = S.h1[:, cols(c)].astype(F32)

    copies = send_table(1, *conv_forward(1, halo_copies))

    halo_y = send_edges(4, 2, S.y.at[1])
    activation0 = push_activation(0)
    back_inner(1, S.y.at[1])
    mean, scale = moments(1, copies)

    copies = send_table(2, *pre_grad(1, mean, scale))
    halo_n = send_edges(2, 1, S.cg)
    back_inner(2, S.cg)
    take_halo(4, halo_y, S.y.at[1])
    back_outer(1, S.y.at[1])
    take_halo(2, halo_n, S.cg)
    back_outer(2, S.cg)
    mean_a, mean_b = take_table(2, copies)
    pass_down(mean, mean_a, mean_b)
    copy = push(S.gbuf.at[0, p], S.gbuf.at[0, p], S.xs.at[1], S.xr.at[1], along(0, q))
    cotangent0 = send_cotangent(0)
    turn_activation(1)
    activation1 = push_activation(1)
    copy.wait_recv()

    act_grad(0)
    copies = send_table(3, *pre_grad(0, None, None))
    conv_grad(1, mean_a, mean_b)
    kernel_grad(1, 0, steps)
    keep_small(1)
    conv_grad(0, *take_table(3, copies))
    halo_copies = send_edges(3, 0, S.cg)
    kernel_grad(0, 0, steps)
    keep_small(0)

    place = x * NY + y
    small = [
        push(
            S.sb.at[lax.rem(x + dx, NX) * NY + lax.rem(y + dy, NY)], S.ar.at[n],
            S.as_.at[n], S.ar_.at[n], plane(dx, dy, p),
        )
        for n, (dx, dy) in enumerate(PLANE[1:])
    ]
    second1 = first_sum(1, activation1 + cotangent1)
    second0 = first_sum(0, activation0 + cotangent0)
    conv_backward(0, lambda: take_halo(3, halo_copies, S.cg))
    for copy in small:
        copy.wait_recv()
    total = S.sb[place]
    for n in range(15):
        total = total + S.ar[n]
    S.zb[z] = total
    small = [
        push(S.zb.at[z], S.zb.at[z], S.zs.at[dz - 1], S.zr.at[dz - 1], depth(dz, p))
        for dz in range(1, NZ)
    ]
    second_sum(1, second1)
    second_sum(0, second0)
    for dz in range(1, NZ):
        from_z = lax.rem(z + NZ - dz, NZ)
        pltpu.make_async_remote_copy(
            src_ref=S.zb.at[from_z], dst_ref=S.zb.at[from_z], send_sem=S.zs.at[dz - 1],
            recv_sem=S.zr.at[dz - 1], device_id=depth(dz, p), device_id_type=MESH,
        ).wait_recv()
    total = S.zb[0]
    for k in range(1, NZ):
        total = total + S.zb[k]
    S.fs[0] = total[0:16]
    S.fs[1] = total[16:32]
    S.fin[p, place] = S.fs[p]
    small = [
        push(S.fs.at[core[rel]], S.fin.at[p, place], S.gs.at[n], S.gr.at[n], plane(dx, dy, core[rel]))
        for n, (dx, dy, rel) in enumerate(GATHER)
    ]
    third_sum()
    for copy in small:
        copy.wait_recv()
    for h in range(2):
        for c in range(TILES):
            at = slice(h * HALF + c * LANE, h * HALF + (c + 1) * LANE)
            for k in range(4):
                t = c * 5 + k
                gk_ref[0, 8 * k : 8 * k + 8, at] = S.fin[h, t // 2, (t % 2) * 8 : (t % 2) * 8 + 8, :]
            t = c * 5 + 4
            gg_ref[:, at] = S.fin[h, t // 2, (t % 2) * 8 : (t % 2) * 8 + 1, :]
            gb_ref[:, at] = S.fin[h, t // 2, (t % 2) * 8 + 1 : (t % 2) * 8 + 2, :]
    for copy in sends:
        copy.wait_send()


def relay_kernel(*refs):
    for k in range(5):
        refs[5 + k][...] = refs[k][...]


def body(*args):
    shapes = scratch()
    names = list(shapes)
    vmem, hbm = pl.BlockSpec(memory_space=pltpu.VMEM), pl.BlockSpec(memory_space=pl.ANY)

    def kern(*refs):
        main_kernel(names, *refs)

    results = pl.pallas_call(
        kern,
        out_shape=(
            jax.ShapeDtypeStruct((1, ROWS, HALF), BF16),
            jax.ShapeDtypeStruct((BLOCK, 1, D), F32),
            jax.ShapeDtypeStruct((1, TAPS, D), F32),
            jax.ShapeDtypeStruct((1, D), F32),
            jax.ShapeDtypeStruct((1, D), F32),
        ),
        in_specs=[hbm, hbm, vmem, hbm, vmem, vmem, vmem],
        out_specs=[vmem] * 5,
        scratch_shapes=list(shapes.values()),
        compiler_params=pltpu.CompilerParams(
            collective_id=0, has_side_effects=True, vmem_limit_bytes=56 << 20
        ),
    )(*args)
    gi, gw, gk, gg, gb = pl.pallas_call(
        relay_kernel,
        out_shape=tuple(jax.ShapeDtypeStruct(r.shape, r.dtype) for r in results),
        in_specs=[vmem] * 5,
        out_specs=[vmem] * 5,
    )(*results)
    return gi, gw.reshape(1, BLOCK, D), gk, gg, gb


def solution(mesh):
    return jax.shard_map(
        body,
        mesh=mesh,
        in_specs=(
            P("dp", "seq", None),
            P("dp", "seq", None),
            P("dp", None),
            P("pipe", None, None),
            P("pipe", None, None),
            P("pipe", None),
            P("pipe", None),
        ),
        out_specs=(
            P("dp", "seq", "pipe"),
            P("pipe", ("seq", "dp"), None),
            P("pipe", None, None),
            P("pipe", None),
            P("pipe", None),
        ),
        check_vma=False,
    )
```

```python
import types

import jax
import jax.numpy as jnp
from jax import lax
from jax.experimental import pallas as pl
from jax.experimental.pallas import tpu as pltpu
from jax.sharding import PartitionSpec as P

EPSILON = 1e-05
MESH = pl.DeviceIdType.MESH
F32, BF16 = jnp.float32, jnp.bfloat16
D, HALF, ROWS, TAPS, RIM, UTTS = 1536, 768, 256, 32, 16, 32
LANE, TILES = 128, 6
NX, NY, NZ = 4, 4, 8
SEQ = NX * NZ
BLOCK = 12
STEP, GROUP = 32, 3
PADDED = ROWS + 2 * RIM

RING = (2, 1, 3, 0)
PLANE = sorted(((dx, dy) for dx in RING for dy in RING), key=lambda at: -min(at[0], 4 - at[0]) - min(at[1], 4 - at[1]))
OFFSETS = [(s, rel) for s in (2, -2, 1, -1, 0) for rel in (0, 1) if (s, rel) != (0, 0)]
DEPTH = (4, 3, 5, 2, 6, 1, 7)
GATHER = [(dx, dy, rel) for dx, dy in PLANE for rel in (0, 1) if (dx, dy, rel) != (0, 0, 0)]


def scratch():
    vm, dma = pltpu.VMEM, pltpu.SemaphoreType.DMA
    return dict(
        hb=vm((ROWS, HALF), BF16),
        gbuf=vm((2, 2, ROWS, HALF), BF16),
        w=vm((2, HALF, D), BF16),
        pst=vm((2, TILES, 40, LANE), F32),
        pb=vm((2, TILES, 40, LANE), F32),
        seg=vm((PADDED, LANE), F32),
        cnt=vm((8, LANE), F32),
        perm=vm((2, HALF, HALF), BF16),
        xf=vm((2, TILES, PADDED, LANE), F32),
        y=vm((2, TILES, PADDED, LANE), F32),
        nrm=vm((2, TILES, ROWS, LANE), F32),
        cb=vm((3, TILES, ROWS, LANE), F32),
        inv=vm((2, ROWS, LANE), F32),
        act=vm((2, ROWS, HALF), BF16),
        ag=vm((2, ROWS, HALF), F32),
        part=vm((ROWS, HALF), F32),
        cg=vm((TILES, PADDED, LANE), F32),
        kga=vm((2, TILES, TAPS, 8, LANE), F32),
        gba=vm((2, 2, TILES, 8, LANE), F32),
        halo=vm((5, 2, RIM, HALF), BF16),
        edge=vm((3, 2, RIM, HALF), BF16),
        hx=vm((2, ROWS, HALF), BF16),
        h1=vm((ROWS, HALF), BF16),
        tab=vm((4, 8, LANE), F32),
        tabr=vm((4, 9, 8, LANE), F32),
        turn=vm((2, 2, HALF, ROWS), BF16),
        ta=vm((2, 4, 2, HALF // 4, ROWS), BF16),
        gq=vm((2, 3, ROWS, HALF), BF16),
        s2=vm((2, 2, HALF // 4, HALF), BF16),
        r2=vm((2, 3, 2, HALF // 16, HALF), BF16),
        t3=vm((HALF // 16 + 8, HALF), F32),
        s3=vm((2, NZ, 16, HALF), BF16),
        r3=vm((NZ, 2, 16, HALF), BF16),
        sb=vm((16, 32, LANE), F32),
        ar=vm((15, 32, LANE), F32),
        zb=vm((NZ, 32, LANE), F32),
        fs=vm((2, 16, LANE), F32),
        fin=vm((2, 16, 16, LANE), F32),
        lsem=dma((4,)),
        hs=dma((5, 2)), hr=dma((5, 2)),
        ws=dma((2,)), wr=dma((2,)),
        xs=dma((2,)), xr=dma((2,)),
        ts=dma((4, 9)), tr=dma((4, 9)),
        tas=dma((2, 4, 2)), tar=dma((2, 4, 2)),
        gqs=dma((2, 4)), gqr=dma((2, 4)),
        s2s=dma((2, 3)), s2r=dma((2, 3)),
        s3s=dma((2, NZ)), s3r=dma((NZ, 2)),
        as_=dma((15,)), ar_=dma((15,)),
        zs=dma((7,)), zr=dma((7,)),
        gs=dma((31,)), gr=dma((31,)),
    )


def fold(v):
    total = v[0:8]
    for r in range(8, v.shape[0], 8):
        total = total + v[r : r + 8]
    return total


def dot(a, b):
    return jnp.dot(a, b, preferred_element_type=F32)


def dot_t(a, b):
    return lax.dot_general(a, b, (((1,), (1,)), ((), ())), preferred_element_type=F32)


def cols(c):
    return slice(c * LANE, (c + 1) * LANE)


def main_kernel(names, hid, up, len_ref, w_hbm, ker_ref, gain_ref, bias_ref,
                gi_ref, gw_ref, gk_ref, gg_ref, gb_ref, *refs):
    S = types.SimpleNamespace(**dict(zip(names, refs)))
    i, p, y = lax.axis_index("seq"), lax.axis_index("pipe"), lax.axis_index("dp")
    q = 1 - p
    z, x = lax.div(i, NX), lax.rem(i, NX)
    own_col = pl.multiple_of(p * HALF, HALF)
    oth_col = pl.multiple_of(q * HALF, HALF)

    def dev(seq, pipe, dp):
        return {"seq": seq, "pipe": pipe, "dp": dp}

    def along(offset, pipe):
        return dev(lax.rem(i + offset + SEQ, SEQ), pipe, y)

    def plane(dx, dy, pipe):
        return dev(z * NX + lax.rem(x + dx, NX), pipe, lax.rem(y + dy, NY))

    def depth(dz, pipe):
        return dev(lax.rem(z + dz, NZ) * NX + x, pipe, y)

    core = (p, q)
    sends = []

    def push(src, dst, ssem, rsem, target):
        copy = pltpu.make_async_remote_copy(
            src_ref=src, dst_ref=dst, send_sem=ssem, recv_sem=rsem,
            device_id=target, device_id_type=MESH,
        )
        copy.start()
        sends.append(copy)
        return copy

    loc = [
        pltpu.make_async_copy(hid.at[0, :, pl.ds(own_col, HALF)], S.hb, S.lsem.at[0]),
        pltpu.make_async_copy(w_hbm.at[0, pl.ds(own_col, HALF), :], S.w.at[p], S.lsem.at[1]),
        pltpu.make_async_copy(up.at[0, :, pl.ds(0, HALF)], S.gbuf.at[1, 0], S.lsem.at[2]),
        pltpu.make_async_copy(up.at[0, :, pl.ds(HALF, HALF)], S.gbuf.at[1, 1], S.lsem.at[3]),
    ]
    for copy in loc:
        copy.start()

    barrier = pltpu.get_barrier_semaphore()
    partners = [along(s, core[rel]) for s, rel in OFFSETS]
    partners += [plane(dx, dy, c) for dx, dy in PLANE if (dx, dy) != (0, 0) for c in core]
    partners += [depth(dz, c) for dz in range(1, NZ) for c in core]
    for target in partners:
        pl.semaphore_signal(barrier, inc=1, device_id=target, device_id_type=MESH)

    for h in range(2):
        for c in range(TILES):
            at = slice(h * HALF + c * LANE, h * HALF + (c + 1) * LANE)
            S.pst[h, c, 0:TAPS, :] = ker_ref[0, :, at]
            row = lax.broadcasted_iota(jnp.int32, (8, LANE), 0)
            S.pst[h, c, TAPS:40, :] = jnp.where(
                row == 0, gain_ref[:, at], jnp.where(row == 1, bias_ref[:, at], 0.0)
            )
    for c in range(TILES):
        S.pb[p, c] = S.pst[p, c]

    lens = len_ref[...].astype(F32)
    io0 = lax.broadcasted_iota(jnp.int32, (UTTS, UTTS), 0)
    io1 = lax.broadcasted_iota(jnp.int32, (UTTS, UTTS), 1)
    lens_col = jnp.sum(jnp.where(io0 == io1, lens, 0.0), axis=1, keepdims=True)
    starts = jnp.sum(jnp.where(io0 < io1, lens_col, 0.0), axis=0, keepdims=True)
    bin_total = jnp.sum(lens, axis=1, keepdims=True)
    frame = (lax.broadcasted_iota(jnp.int32, (PADDED, UTTS), 0) + (i * ROWS - RIM)).astype(F32)
    owner = jnp.sum(jnp.where(starts <= frame, 1.0, 0.0), axis=1, keepdims=True) - 1.0
    inside = (frame[:, 0:1] >= 0.0) & (frame[:, 0:1] < bin_total)
    S.seg[...] = jnp.broadcast_to(jnp.where(inside, owner, -2.0), (PADDED, LANE))
    S.cnt[...] = jnp.full((8, LANE), float(D), F32)
    S.cnt[0:1, 0:UTTS] = lens * float(D)

    r = lax.broadcasted_iota(jnp.int32, (HALF, LANE), 0).astype(F32)
    blk = jnp.floor((r + 0.5) / BLOCK)
    word = r - BLOCK * blk
    b4 = jnp.floor((blk + 0.5) / 4.0)
    dig0 = blk - 4.0 * b4
    dig2 = jnp.floor((b4 + 0.5) / 4.0)
    dig1 = b4 - 4.0 * dig2
    lane = lax.broadcasted_iota(jnp.int32, (HALF, LANE), 1).astype(F32)
    for path, (yy, xx) in enumerate(((dig2, dig1), (dig1, dig2))):
        nat = ((dig0 * 4.0 + xx) * 4.0 + yy) * BLOCK + word
        for c in range(TILES):
            S.perm[path, :, cols(c)] = jnp.where(nat == lane + float(c * LANE), 1.0, 0.0).astype(BF16)

    S.kga[...] = jnp.zeros(S.kga.shape, F32)
    S.sb[15] = jnp.zeros((32, LANE), F32)
    S.t3[HALF // 16 :, :] = jnp.zeros((8, HALF), F32)

    pl.semaphore_wait(barrier, len(partners))

    def send_halo(rnd, first, last):
        return [
            push(last, S.halo.at[rnd, 0], S.hs.at[rnd, 0], S.hr.at[rnd, 0], along(1, p)),
            push(first, S.halo.at[rnd, 1], S.hs.at[rnd, 1], S.hr.at[rnd, 1], along(-1, p)),
        ]

    def take_halo(rnd, copies, dst):
        for copy in copies:
            copy.wait_recv()
        for c in range(TILES):
            dst[c, 0:RIM, :] = S.halo[rnd, 0, :, cols(c)].astype(F32)
            dst[c, RIM + ROWS :, :] = S.halo[rnd, 1, :, cols(c)].astype(F32)

    halo_copies = send_halo(
        0,
        hid.at[0, pl.ds(0, RIM), pl.ds(own_col, HALF)],
        hid.at[0, pl.ds(ROWS - RIM, RIM), pl.ds(own_col, HALF)],
    )
    par_copy = push(S.pst.at[q], S.pb.at[p], S.ws.at[0], S.wr.at[0], along(0, q))
    w_copy = push(
        w_hbm.at[0, pl.ds(oth_col, HALF), :], S.w.at[p], S.ws.at[1], S.wr.at[1], along(0, q)
    )

    loc[0].wait()
    for c in range(TILES):
        S.xf[0, c, RIM : RIM + ROWS, :] = S.hb[:, cols(c)].astype(F32)

    steps = ROWS // STEP
    lane_id = lax.broadcasted_iota(jnp.int32, (STEP, LANE), 1).astype(F32)

    def base_of(b):
        return pl.multiple_of(b * STEP, STEP)

    def member(base):
        return S.seg[pl.ds(base + RIM, STEP), :] == lane_id

    def table_add(onehot, v):
        return fold(jnp.where(onehot, jnp.sum(v, axis=1, keepdims=True), 0.0))

    def pick(onehot, row):
        return jnp.sum(jnp.where(onehot, row, 0.0), axis=1, keepdims=True)

    zero_tab = jnp.zeros((8, LANE), F32)

    def send_table(rnd, t1, t2):
        row = lax.broadcasted_iota(jnp.int32, (8, LANE), 0)
        t1 = jnp.sum(t1, axis=0, keepdims=True)
        t2 = jnp.sum(t2, axis=0, keepdims=True)
        S.tab[rnd] = jnp.where(row == 0, t1, jnp.where(row == 1, t2, 0.0))
        return [
            push(S.tab.at[rnd], S.tabr.at[rnd, n], S.ts.at[rnd, n], S.tr.at[rnd, n], along(s, core[rel]))
            for n, (s, rel) in enumerate(OFFSETS)
        ]

    def take_table(rnd, copies):
        total = S.tab[rnd]
        for copy in copies:
            copy.wait_recv()
        for n in range(9):
            total = total + S.tabr[rnd, n]
        count = S.cnt[0:1, :]
        return total[0:1] / count, total[1:2] / count

    def inside_first(step, carry, then):
        carry = lax.fori_loop(1, steps - 1, step, carry)
        then()
        return lax.fori_loop(0, 2, lambda b, held: step(b * (steps - 1), held), carry)

    def conv_forward(s, copies):
        def step(b, carry):
            t1, t2 = carry
            base = base_of(b)
            centre = S.seg[pl.ds(base + RIM, STEP), :]
            first = second = jnp.zeros((STEP, LANE), F32)
            for g in range(0, TILES, GROUP):
                acc = [jnp.zeros((STEP, LANE), F32) for _ in range(GROUP)]
                for j in range(TAPS):
                    same = S.seg[pl.ds(base + j + 1, STEP), :] == centre
                    for c in range(GROUP):
                        window = S.xf[s, g + c, pl.ds(base + j + 1, STEP), :]
                        acc[c] = acc[c] + jnp.where(same, window * S.pb[s, g + c, j : j + 1, :], 0.0)
                for c in range(GROUP):
                    S.y[s, g + c, pl.ds(base + RIM, STEP), :] = acc[c]
                    first = first + acc[c]
                    second = second + acc[c] * acc[c]
            onehot = member(base)
            return t1 + table_add(onehot, first), t2 + table_add(onehot, second)

        return inside_first(step, (zero_tab, zero_tab), lambda: take_halo(s, copies, S.xf.at[s]))

    def moments(rnd, copies):
        mean, square = take_table(rnd, copies)
        spread = jnp.maximum(square - mean * mean, 0.0)
        return mean, lax.rsqrt(spread + EPSILON)

    def normalize(s, base, onehot, mean, scale):
        m, v = pick(onehot, mean), pick(onehot, scale)
        S.inv[s, pl.ds(base, STEP), :] = jnp.broadcast_to(v, (STEP, LANE))
        return m, v

    def activate(s, base, c, normed):
        gain, bias = S.pb[s, c, TAPS : TAPS + 1, :], S.pb[s, c, TAPS + 1 : TAPS + 2, :]
        pre = normed * gain + bias
        sig = jax.nn.sigmoid(pre)
        return gain, pre, sig

    def act_grad(s):
        S.ag[s] = dot_t(S.gbuf[s, 0], S.w[s, :, 0:HALF]) + dot_t(S.gbuf[s, 1], S.w[s, :, HALF:])

    def pre_grad(s, mean, scale):
        def step(b, carry):
            t1, t2, gains, biases = carry
            base = base_of(b)
            onehot = member(base)
            at = pl.ds(base, STEP)
            if s == 1:
                m, v = normalize(1, base, onehot, mean, scale)
            first = second = jnp.zeros((STEP, LANE), F32)
            new_gains, new_biases = [], []
            for c in range(TILES):
                if s == 1:
                    normed = (S.y[1, c, pl.ds(base + RIM, STEP), :] - m) * v
                    S.nrm[1, c, at, :] = normed
                else:
                    normed = S.nrm[0, c, at, :]
                gain, pre, sig = activate(s, base, c, normed)
                if s == 1:
                    S.act[1, at, cols(c)] = (pre * sig).astype(BF16)
                grad = S.ag[s, at, cols(c)] * sig * (1.0 + pre * (1.0 - sig))
                scaled = grad * gain
                S.ag[s, at, cols(c)] = scaled
                if s == 1:
                    S.cg[c, pl.ds(base + RIM, STEP), :] = scaled
                first = first + scaled
                second = second + scaled * normed
                new_gains.append(gains[c] + fold(grad * normed))
                new_biases.append(biases[c] + fold(grad))
            return (t1 + table_add(onehot, first), t2 + table_add(onehot, second),
                    tuple(new_gains), tuple(new_biases))

        zeros = tuple(zero_tab for _ in range(TILES))
        t1, t2, gains, biases = lax.fori_loop(0, steps, step, (zero_tab, zero_tab, zeros, zeros))
        for c in range(TILES):
            S.gba[s, 0, c] = gains[c]
            S.gba[s, 1, c] = biases[c]
        return t1, t2

    def conv_grad(s, mean_a, mean_b):
        def step(b, _):
            base = base_of(b)
            onehot = member(base)
            ca, cb = pick(onehot, mean_a), pick(onehot, mean_b)
            at = pl.ds(base, STEP)
            v = S.inv[s, at, :]
            for c in range(TILES):
                S.cg[c, pl.ds(base + RIM, STEP), :] = v * (S.ag[s, at, cols(c)] - ca - S.nrm[s, c, at, :] * cb)
            return 0

        lax.fori_loop(0, steps, step, 0)

    def send_edges(rnd, k, src):
        for c in range(TILES):
            S.edge[k, 0, :, cols(c)] = src[c, RIM : 2 * RIM, :].astype(BF16)
            S.edge[k, 1, :, cols(c)] = src[c, ROWS : ROWS + RIM, :].astype(BF16)
        return send_halo(rnd, S.edge.at[k, 0], S.edge.at[k, 1])

    def back_step(k, src):
        def step(b, _):
            base = base_of(b)
            centre = S.seg[pl.ds(base + RIM, STEP), :]
            for g in range(0, TILES, GROUP):
                acc = [jnp.zeros((STEP, LANE), F32) for _ in range(GROUP)]
                for j in range(TAPS):
                    same = S.seg[pl.ds(base + TAPS - 1 - j, STEP), :] == centre
                    for c in range(GROUP):
                        term = S.pb[1, g + c, j : j + 1, :]
                        if src is not None:
                            term = src[g + c, pl.ds(base + TAPS - 1 - j, STEP), :] * term
                        acc[c] = acc[c] + jnp.where(same, term, 0.0)
                for c in range(GROUP):
                    S.cb[k, g + c, pl.ds(base, STEP), :] = acc[c]
            return 0

        return step

    def back_inner(k, src):
        lax.fori_loop(1, steps - 1, back_step(k, src), 0)

    def back_outer(k, src):
        lax.fori_loop(0, 2, lambda b, _: back_step(k, src)(b * (steps - 1), 0), 0)

    def pass_down(mean, mean_a, mean_b):
        def step(b, _):
            base = base_of(b)
            onehot = member(base)
            at = pl.ds(base, STEP)
            v = S.inv[1, at, :]
            slope = pick(onehot, mean_b) * v
            level = pick(onehot, mean_a) - slope * pick(onehot, mean)
            for c in range(TILES):
                back = v * (S.cb[2, c, at, :] - level * S.cb[0, c, at, :] - slope * S.cb[1, c, at, :])
                S.gbuf[0, p, at, cols(c)] = (S.gbuf[1, p, at, cols(c)].astype(F32) + back).astype(BF16)
            return 0

        lax.fori_loop(0, steps, step, 0)

    def conv_backward(s, then):
        def step(b, _):
            base = base_of(b)
            at = pl.ds(base, STEP)
            centre = S.seg[pl.ds(base + RIM, STEP), :]
            for g in range(0, TILES, GROUP):
                acc = [jnp.zeros((STEP, LANE), F32) for _ in range(GROUP)]
                for j in range(TAPS):
                    same = S.seg[pl.ds(base + TAPS - 1 - j, STEP), :] == centre
                    for c in range(GROUP):
                        window = S.cg[g + c, pl.ds(base + TAPS - 1 - j, STEP), :]
                        acc[c] = acc[c] + jnp.where(same, window * S.pb[s, g + c, j : j + 1, :], 0.0)
                for c in range(GROUP):
                    passed = S.gbuf[s, p, at, cols(g + c)].astype(F32) + acc[c]
                    gi_ref[0, at, cols(g + c)] = passed.astype(BF16)
            return 0

        inside_first(step, 0, then)

    def kernel_grad(s, low, high):
        def step(b, _):
            base = base_of(b)
            centre = S.seg[pl.ds(base + RIM, STEP), :]
            for g in range(0, TILES, GROUP):
                mine = [S.cg[g + c, pl.ds(base + RIM, STEP), :] for c in range(GROUP)]
                for j in range(TAPS):
                    same = S.seg[pl.ds(base + j + 1, STEP), :] == centre
                    for c in range(GROUP):
                        window = S.xf[s, g + c, pl.ds(base + j + 1, STEP), :]
                        S.kga[s, g + c, j] += fold(jnp.where(same, window * mine[c], 0.0))
            return 0

        lax.fori_loop(low, high, step, 0)

    def keep_small(s):
        row = lax.broadcasted_iota(jnp.int32, (8, LANE), 0)
        for c in range(TILES):
            for k in range(4):
                t = c * 5 + k
                at = slice(s * 16 + (t % 2) * 8, s * 16 + (t % 2) * 8 + 8)
                S.sb[t // 2, at, :] = jnp.sum(S.kga[s, c, 8 * k : 8 * k + 8], axis=1)
            t = c * 5 + 4
            at = slice(s * 16 + (t % 2) * 8, s * 16 + (t % 2) * 8 + 8)
            gsum = jnp.sum(S.gba[s, 0, c], axis=0, keepdims=True)
            bsum = jnp.sum(S.gba[s, 1, c], axis=0, keepdims=True)
            S.sb[t // 2, at, :] = jnp.where(row == 0, gsum, jnp.where(row == 1, bsum, 0.0))

    q1, q2 = HALF // 4, HALF // 16
    first_place = jnp.where(p == 0, y, x)
    second_place = jnp.where(p == 0, x, y)

    def first_ring(d, path):
        return plane(d * path, d * (1 - path), path)

    def second_ring(d):
        return plane(d * (1 - p), d * p, p)

    def send_cotangent(s, distances):
        return [
            push(S.gbuf.at[s, p], S.gq.at[s, d - 1], S.gqs.at[s, d - 1], S.gqr.at[s, d - 1], first_ring(d, p))
            for d in distances
        ]

    def forward_cotangent(s):
        half = ROWS // 2
        return [
            push(
                S.gq.at[s, d - 1, pl.ds(at, half), :], S.gq.at[s, 1, pl.ds(at, half), :],
                S.gqs.at[s, n], S.gqr.at[s, n], first_ring(d, p),
            )
            for d, at, n in ((1, 0, 1), (3, half, 3))
        ]

    def turn_activation(s):
        def step(k, _):
            at = pl.ds(pl.multiple_of(k * 256, 256), 256)
            for path in range(2):
                S.turn[s, path, at, :] = dot_t(S.perm[path, at, :], S.act[s]).astype(BF16)
            return 0

        lax.fori_loop(0, HALF // 256, step, 0)

    def push_activation(s):
        copies = []
        for d in range(4):
            for rel in range(2):
                path = core[rel]
                place = lax.rem(jnp.where(path == 0, y, x) + d, 4)
                rows = pl.ds(pl.multiple_of(place * q1, q1), q1)
                if (d, rel) == (0, 0):
                    S.ta[s, 0, p] = S.turn[s, p, rows, :]
                else:
                    copies.append(push(
                        S.turn.at[s, path, rows, :], S.ta.at[s, d, p], S.tas.at[s, d, rel], S.tar.at[s, d, rel],
                        first_ring(d, path),
                    ))
        return copies

    def first_sum(s, copies):
        for copy in copies:
            copy.wait_recv()
        for h in range(2):
            total = dot(S.ta[s, 0, h], S.gbuf[s, p])
            for d in range(3):
                total = total + dot(S.ta[s, d + 1, h], S.gq[s, d])
            S.s2[s, h] = total.astype(BF16)
        return [
            push(
                S.s2.at[s, :, pl.ds(pl.multiple_of(lax.rem(second_place + d, 4) * q2, q2), q2), :],
                S.r2.at[s, d - 1], S.s2s.at[s, d - 1], S.s2r.at[s, d - 1], second_ring(d),
            )
            for d in (1, 3, 2)
        ]

    def third_copy(s, dz):
        rel = jnp.where(p == s, 0, 1)
        return pltpu.make_async_remote_copy(
            src_ref=S.s3.at[s, lax.rem(z + dz, NZ)], dst_ref=S.r3.at[dz, rel], send_sem=S.s3s.at[s, dz],
            recv_sem=S.s3r.at[dz, rel], device_id=depth(dz, s), device_id_type=MESH,
        )

    def second_sum(s, copies):
        for copy in copies:
            copy.wait_recv()
        mine = pl.ds(pl.multiple_of(second_place * q2, q2), q2)
        for h in range(2):
            total = S.s2[s, h, mine, :].astype(F32)
            for d in range(3):
                total = total + S.r2[s, d, h].astype(F32)
            S.t3[0:q2, :] = total
            for k in range(4):
                S.s3[s, 4 * h + k] = S.t3[BLOCK * k : BLOCK * k + 16, :].astype(BF16)
        for dz in DEPTH:
            third_copy(s, dz).start()

        @pl.when(p != s)
        def _():
            third_copy(s, 0).start()

        @pl.when(p == s)
        def _():
            S.r3[0, 0] = S.s3[s, z]

    def third_sum():
        for s in range(2):
            for dz in range(1, NZ):
                third_copy(s, dz).wait_send()

            @pl.when(p != s)
            def _():
                third_copy(s, 0).wait_send()
        for rel, at in ((0, own_col), (1, oth_col)):
            total = jnp.zeros((16, HALF), F32)
            for dz in range(NZ):
                if (dz, rel) != (0, 0):
                    pltpu.make_async_remote_copy(
                        src_ref=S.s3.at[0, 0], dst_ref=S.r3.at[dz, rel], send_sem=S.s3s.at[0, 0],
                        recv_sem=S.s3r.at[dz, rel], device_id=along(0, q), device_id_type=MESH,
                    ).wait_recv()
                total = total + S.r3[dz, rel].astype(F32)
            for k in range(BLOCK):
                gw_ref[k, :, pl.ds(at, HALF)] = total[k : k + 1]

    loc[2].wait()
    loc[3].wait()
    cotangent1 = send_cotangent(1, (2,))
    par_copy.wait_recv()
    copies = send_table(0, *conv_forward(0, halo_copies))
    lax.fori_loop(0, steps, back_step(0, None), 0)
    loc[1].wait()
    w_copy.wait_recv()
    act_grad(1)
    mean, scale = moments(0, copies)
    cotangent1 += send_cotangent(1, (1, 3))

    def norm_step(b, _):
        base = base_of(b)
        m, v = normalize(0, base, member(base), mean, scale)
        for c in range(TILES):
            normed = (S.y[0, c, pl.ds(base + RIM, STEP), :] - m) * v
            S.nrm[0, c, pl.ds(base, STEP), :] = normed
            _, pre, sig = activate(0, base, c, normed)
            S.act[0, pl.ds(base, STEP), cols(c)] = (pre * sig).astype(BF16)
        return 0

    lax.fori_loop(0, steps, norm_step, 0)
    S.hx[0] = dot(S.act[0], S.w[0, :, pl.ds(oth_col, HALF)]).astype(BF16)
    copy = push(S.hx.at[0], S.hx.at[1], S.xs.at[0], S.xr.at[0], along(0, q))
    S.part[...] = dot(S.act[0], S.w[0, :, pl.ds(own_col, HALF)])
    turn_activation(0)
    copy.wait_recv()

    def out_step(b, _):
        base = base_of(b)
        at = pl.ds(base, STEP)
        S.h1[at, :] = (S.hb[at, :].astype(F32) + (S.part[at, :] + S.hx[1, at, :].astype(F32))).astype(BF16)
        return 0

    lax.fori_loop(0, steps, out_step, 0)
    halo_copies = send_halo(1, S.h1.at[pl.ds(0, RIM), :], S.h1.at[pl.ds(ROWS - RIM, RIM), :])
    for c in range(TILES):
        S.xf[1, c, RIM : RIM + ROWS, :] = S.h1[:, cols(c)].astype(F32)

    copies = send_table(1, *conv_forward(1, halo_copies))

    halo_y = send_edges(4, 2, S.y.at[1])
    activation0 = push_activation(0)
    back_inner(1, S.y.at[1])
    mean, scale = moments(1, copies)

    copies = send_table(2, *pre_grad(1, mean, scale))
    halo_n = send_edges(2, 1, S.cg)
    back_inner(2, S.cg)
    take_halo(4, halo_y, S.y.at[1])
    back_outer(1, S.y.at[1])
    take_halo(2, halo_n, S.cg)
    back_outer(2, S.cg)
    mean_a, mean_b = take_table(2, copies)
    pass_down(mean, mean_a, mean_b)
    copy = push(S.gbuf.at[0, p], S.gbuf.at[0, p], S.xs.at[1], S.xr.at[1], along(0, q))
    cotangent0 = send_cotangent(0, (1, 3))
    turn_activation(1)
    copy.wait_recv()

    act_grad(0)
    copies = send_table(3, *pre_grad(0, None, None))
    activation1 = push_activation(1)
    conv_grad(1, mean_a, mean_b)
    kernel_grad(1, 0, steps)
    keep_small(1)
    mean_a, mean_b = take_table(3, copies)
    for copy in cotangent0:
        copy.wait_recv()
    cotangent0 = forward_cotangent(0)
    conv_grad(0, mean_a, mean_b)
    halo_copies = send_edges(3, 0, S.cg)
    kernel_grad(0, 0, steps)
    keep_small(0)

    place = x * NY + y
    small = [
        push(
            S.sb.at[lax.rem(x + dx, NX) * NY + lax.rem(y + dy, NY)], S.ar.at[n],
            S.as_.at[n], S.ar_.at[n], plane(dx, dy, p),
        )
        for n, (dx, dy) in enumerate(PLANE[:-1])
    ]
    second1 = first_sum(1, activation1 + cotangent1)
    second0 = first_sum(0, activation0 + cotangent0)
    conv_backward(0, lambda: take_halo(3, halo_copies, S.cg))
    for copy in small:
        copy.wait_recv()
    total = S.sb[place]
    for n in range(15):
        total = total + S.ar[n]
    S.zb[z] = total
    small = [
        push(S.zb.at[z], S.zb.at[z], S.zs.at[dz - 1], S.zr.at[dz - 1], depth(dz, p))
        for dz in DEPTH
    ]
    second_sum(1, second1)
    second_sum(0, second0)
    for dz in range(1, NZ):
        from_z = lax.rem(z + NZ - dz, NZ)
        pltpu.make_async_remote_copy(
            src_ref=S.zb.at[from_z], dst_ref=S.zb.at[from_z], send_sem=S.zs.at[dz - 1],
            recv_sem=S.zr.at[dz - 1], device_id=depth(dz, p), device_id_type=MESH,
        ).wait_recv()
    total = S.zb[0]
    for k in range(1, NZ):
        total = total + S.zb[k]
    S.fs[0] = total[0:16]
    S.fs[1] = total[16:32]
    S.fin[p, place] = S.fs[p]
    small = [
        push(S.fs.at[core[rel]], S.fin.at[p, place], S.gs.at[n], S.gr.at[n], plane(dx, dy, core[rel]))
        for n, (dx, dy, rel) in enumerate(GATHER)
    ]
    third_sum()
    for copy in small:
        copy.wait_recv()
    for h in range(2):
        for c in range(TILES):
            at = slice(h * HALF + c * LANE, h * HALF + (c + 1) * LANE)
            for k in range(4):
                t = c * 5 + k
                gk_ref[0, 8 * k : 8 * k + 8, at] = S.fin[h, t // 2, (t % 2) * 8 : (t % 2) * 8 + 8, :]
            t = c * 5 + 4
            gg_ref[:, at] = S.fin[h, t // 2, (t % 2) * 8 : (t % 2) * 8 + 1, :]
            gb_ref[:, at] = S.fin[h, t // 2, (t % 2) * 8 + 1 : (t % 2) * 8 + 2, :]
    for copy in sends:
        copy.wait_send()


def relay_kernel(*refs):
    for k in range(5):
        refs[5 + k][...] = refs[k][...]


def body(*args):
    shapes = scratch()
    names = list(shapes)
    vmem, hbm = pl.BlockSpec(memory_space=pltpu.VMEM), pl.BlockSpec(memory_space=pl.ANY)

    def kern(*refs):
        main_kernel(names, *refs)

    results = pl.pallas_call(
        kern,
        out_shape=(
            jax.ShapeDtypeStruct((1, ROWS, HALF), BF16),
            jax.ShapeDtypeStruct((BLOCK, 1, D), F32),
            jax.ShapeDtypeStruct((1, TAPS, D), F32),
            jax.ShapeDtypeStruct((1, D), F32),
            jax.ShapeDtypeStruct((1, D), F32),
        ),
        in_specs=[hbm, hbm, vmem, hbm, vmem, vmem, vmem],
        out_specs=[vmem] * 5,
        scratch_shapes=list(shapes.values()),
        compiler_params=pltpu.CompilerParams(
            collective_id=0, has_side_effects=True, vmem_limit_bytes=56 << 20
        ),
    )(*args)
    gi, gw, gk, gg, gb = pl.pallas_call(
        relay_kernel,
        out_shape=tuple(jax.ShapeDtypeStruct(r.shape, r.dtype) for r in results),
        in_specs=[vmem] * 5,
        out_specs=[vmem] * 5,
    )(*results)
    return gi, gw.reshape(1, BLOCK, D), gk, gg, gb


def solution(mesh):
    return jax.shard_map(
        body,
        mesh=mesh,
        in_specs=(
            P("dp", "seq", None),
            P("dp", "seq", None),
            P("dp", None),
            P("pipe", None, None),
            P("pipe", None, None),
            P("pipe", None),
            P("pipe", None),
        ),
        out_specs=(
            P("dp", "seq", "pipe"),
            P("pipe", ("seq", "dp"), None),
            P("pipe", None, None),
            P("pipe", None),
            P("pipe", None),
        ),
        check_vma=False,
    )
```

```python
import types

import jax
import jax.numpy as jnp
from jax import lax
from jax.experimental import pallas as pl
from jax.experimental.pallas import tpu as pltpu
from jax.sharding import PartitionSpec as P

EPSILON = 1e-05
MESH = pl.DeviceIdType.MESH
F32, BF16 = jnp.float32, jnp.bfloat16
D, HALF, ROWS, TAPS, RIM, UTTS = 1536, 768, 256, 32, 16, 32
LANE, TILES = 128, 6
NX, NY, NZ = 4, 4, 8
SEQ = NX * NZ
BLOCK = 12
STEP, GROUP = 32, 3
PADDED = ROWS + 2 * RIM

RING = (2, 1, 3, 0)
PLANE = sorted(((dx, dy) for dx in RING for dy in RING), key=lambda at: -min(at[0], 4 - at[0]) - min(at[1], 4 - at[1]))
OFFSETS = [(s, rel) for s in (2, -2, 1, -1, 0) for rel in (0, 1) if (s, rel) != (0, 0)]
DEPTH = (4, 3, 5, 2, 6, 1, 7)
GATHER = [(dx, dy, rel) for dx, dy in PLANE for rel in (0, 1) if (dx, dy, rel) != (0, 0, 0)]


def scratch():
    vm, dma = pltpu.VMEM, pltpu.SemaphoreType.DMA
    return dict(
        hb=vm((ROWS, HALF), BF16),
        gbuf=vm((2, 2, ROWS, HALF), BF16),
        w=vm((2, HALF, D), BF16),
        pst=vm((2, TILES, 40, LANE), F32),
        pb=vm((2, TILES, 40, LANE), F32),
        seg=vm((PADDED, LANE), F32),
        cnt=vm((8, LANE), F32),
        perm=vm((2, HALF, HALF), BF16),
        xf=vm((2, TILES, PADDED, LANE), F32),
        y=vm((2, TILES, PADDED, LANE), F32),
        nrm=vm((2, TILES, ROWS, LANE), F32),
        cb=vm((3, TILES, ROWS, LANE), F32),
        inv=vm((2, ROWS, LANE), F32),
        act=vm((2, ROWS, HALF), BF16),
        ag=vm((2, ROWS, HALF), F32),
        part=vm((ROWS, HALF), F32),
        cg=vm((TILES, PADDED, LANE), F32),
        kga=vm((2, TILES, TAPS, 8, LANE), F32),
        gba=vm((2, 2, TILES, 8, LANE), F32),
        halo=vm((5, 2, RIM, HALF), BF16),
        edge=vm((3, 2, RIM, HALF), BF16),
        hx=vm((2, ROWS, HALF), BF16),
        h1=vm((ROWS, HALF), BF16),
        tab=vm((4, 8, LANE), F32),
        tabr=vm((4, 9, 8, LANE), F32),
        turn=vm((2, 2, HALF, ROWS), BF16),
        ta=vm((2, 4, 2, HALF // 4, ROWS), BF16),
        gq=vm((2, 3, ROWS, HALF), BF16),
        s2=vm((2, 2, HALF // 4, HALF), BF16),
        r2=vm((2, 3, 2, HALF // 16, HALF), BF16),
        t3=vm((HALF // 16 + 8, HALF), F32),
        s3=vm((2, NZ, 16, HALF), BF16),
        r3=vm((NZ, 2, 16, HALF), BF16),
        sb=vm((16, 32, LANE), F32),
        ar=vm((15, 32, LANE), F32),
        zb=vm((NZ, 32, LANE), F32),
        fs=vm((2, 16, LANE), F32),
        fin=vm((2, 16, 16, LANE), F32),
        lsem=dma((4,)),
        hs=dma((5, 2)), hr=dma((5, 2)),
        ws=dma((2,)), wr=dma((2,)),
        xs=dma((2,)), xr=dma((2,)),
        ts=dma((4, 9)), tr=dma((4, 9)),
        tas=dma((2, 4, 2)), tar=dma((2, 4, 2)),
        gqs=dma((2, 4)), gqr=dma((2, 4)),
        s2s=dma((2, 3)), s2r=dma((2, 3)),
        s3s=dma((2, NZ)), s3r=dma((NZ, 2)),
        as_=dma((15,)), ar_=dma((15,)),
        zs=dma((7,)), zr=dma((7,)),
        gs=dma((31,)), gr=dma((31,)),
    )


def fold(v):
    total = v[0:8]
    for r in range(8, v.shape[0], 8):
        total = total + v[r : r + 8]
    return total


def dot(a, b):
    return jnp.dot(a, b, preferred_element_type=F32)


def dot_t(a, b):
    return lax.dot_general(a, b, (((1,), (1,)), ((), ())), preferred_element_type=F32)


def cols(c):
    return slice(c * LANE, (c + 1) * LANE)


def main_kernel(names, hid, up, len_ref, w_hbm, ker_ref, gain_ref, bias_ref,
                gi_ref, gw_ref, gk_ref, gg_ref, gb_ref, *refs):
    S = types.SimpleNamespace(**dict(zip(names, refs)))
    i, p, y = lax.axis_index("seq"), lax.axis_index("pipe"), lax.axis_index("dp")
    q = 1 - p
    z, x = lax.div(i, NX), lax.rem(i, NX)
    own_col = pl.multiple_of(p * HALF, HALF)
    oth_col = pl.multiple_of(q * HALF, HALF)

    def dev(seq, pipe, dp):
        return {"seq": seq, "pipe": pipe, "dp": dp}

    def along(offset, pipe):
        return dev(lax.rem(i + offset + SEQ, SEQ), pipe, y)

    def plane(dx, dy, pipe):
        return dev(z * NX + lax.rem(x + dx, NX), pipe, lax.rem(y + dy, NY))

    def depth(dz, pipe):
        return dev(lax.rem(z + dz, NZ) * NX + x, pipe, y)

    core = (p, q)
    sends = []

    def push(src, dst, ssem, rsem, target):
        copy = pltpu.make_async_remote_copy(
            src_ref=src, dst_ref=dst, send_sem=ssem, recv_sem=rsem,
            device_id=target, device_id_type=MESH,
        )
        copy.start()
        sends.append(copy)
        return copy

    loc = [
        pltpu.make_async_copy(hid.at[0, :, pl.ds(own_col, HALF)], S.hb, S.lsem.at[0]),
        pltpu.make_async_copy(w_hbm.at[0, pl.ds(own_col, HALF), :], S.w.at[p], S.lsem.at[1]),
        pltpu.make_async_copy(up.at[0, :, pl.ds(0, HALF)], S.gbuf.at[1, 0], S.lsem.at[2]),
        pltpu.make_async_copy(up.at[0, :, pl.ds(HALF, HALF)], S.gbuf.at[1, 1], S.lsem.at[3]),
    ]
    for copy in loc:
        copy.start()

    barrier = pltpu.get_barrier_semaphore()
    partners = [along(s, core[rel]) for s, rel in OFFSETS]
    partners += [plane(dx, dy, c) for dx, dy in PLANE if (dx, dy) != (0, 0) for c in core]
    partners += [depth(dz, c) for dz in range(1, NZ) for c in core]
    for target in partners:
        pl.semaphore_signal(barrier, inc=1, device_id=target, device_id_type=MESH)

    for h in range(2):
        for c in range(TILES):
            at = slice(h * HALF + c * LANE, h * HALF + (c + 1) * LANE)
            S.pst[h, c, 0:TAPS, :] = ker_ref[0, :, at]
            row = lax.broadcasted_iota(jnp.int32, (8, LANE), 0)
            S.pst[h, c, TAPS:40, :] = jnp.where(
                row == 0, gain_ref[:, at], jnp.where(row == 1, bias_ref[:, at], 0.0)
            )
    for c in range(TILES):
        S.pb[p, c] = S.pst[p, c]

    lens = len_ref[...].astype(F32)
    io0 = lax.broadcasted_iota(jnp.int32, (UTTS, UTTS), 0)
    io1 = lax.broadcasted_iota(jnp.int32, (UTTS, UTTS), 1)
    lens_col = jnp.sum(jnp.where(io0 == io1, lens, 0.0), axis=1, keepdims=True)
    starts = jnp.sum(jnp.where(io0 < io1, lens_col, 0.0), axis=0, keepdims=True)
    bin_total = jnp.sum(lens, axis=1, keepdims=True)
    frame = (lax.broadcasted_iota(jnp.int32, (PADDED, UTTS), 0) + (i * ROWS - RIM)).astype(F32)
    owner = jnp.sum(jnp.where(starts <= frame, 1.0, 0.0), axis=1, keepdims=True) - 1.0
    inside = (frame[:, 0:1] >= 0.0) & (frame[:, 0:1] < bin_total)
    S.seg[...] = jnp.broadcast_to(jnp.where(inside, owner, -2.0), (PADDED, LANE))
    S.cnt[...] = jnp.full((8, LANE), float(D), F32)
    S.cnt[0:1, 0:UTTS] = lens * float(D)

    r = lax.broadcasted_iota(jnp.int32, (HALF, LANE), 0).astype(F32)
    blk = jnp.floor((r + 0.5) / BLOCK)
    word = r - BLOCK * blk
    b4 = jnp.floor((blk + 0.5) / 4.0)
    dig0 = blk - 4.0 * b4
    dig2 = jnp.floor((b4 + 0.5) / 4.0)
    dig1 = b4 - 4.0 * dig2
    lane = lax.broadcasted_iota(jnp.int32, (HALF, LANE), 1).astype(F32)
    for path, (yy, xx) in enumerate(((dig2, dig1), (dig1, dig2))):
        nat = ((dig0 * 4.0 + xx) * 4.0 + yy) * BLOCK + word
        for c in range(TILES):
            S.perm[path, :, cols(c)] = jnp.where(nat == lane + float(c * LANE), 1.0, 0.0).astype(BF16)

    S.kga[...] = jnp.zeros(S.kga.shape, F32)
    S.sb[15] = jnp.zeros((32, LANE), F32)
    S.t3[HALF // 16 :, :] = jnp.zeros((8, HALF), F32)

    pl.semaphore_wait(barrier, len(partners))

    def send_halo(rnd, first, last):
        return [
            push(last, S.halo.at[rnd, 0], S.hs.at[rnd, 0], S.hr.at[rnd, 0], along(1, p)),
            push(first, S.halo.at[rnd, 1], S.hs.at[rnd, 1], S.hr.at[rnd, 1], along(-1, p)),
        ]

    def take_halo(rnd, copies, dst):
        for copy in copies:
            copy.wait_recv()
        for c in range(TILES):
            dst[c, 0:RIM, :] = S.halo[rnd, 0, :, cols(c)].astype(F32)
            dst[c, RIM + ROWS :, :] = S.halo[rnd, 1, :, cols(c)].astype(F32)

    halo_copies = send_halo(
        0,
        hid.at[0, pl.ds(0, RIM), pl.ds(own_col, HALF)],
        hid.at[0, pl.ds(ROWS - RIM, RIM), pl.ds(own_col, HALF)],
    )
    par_copy = push(S.pst.at[q], S.pb.at[p], S.ws.at[0], S.wr.at[0], along(0, q))
    w_copy = push(
        w_hbm.at[0, pl.ds(oth_col, HALF), :], S.w.at[p], S.ws.at[1], S.wr.at[1], along(0, q)
    )

    loc[0].wait()
    for c in range(TILES):
        S.xf[0, c, RIM : RIM + ROWS, :] = S.hb[:, cols(c)].astype(F32)

    steps = ROWS // STEP
    lane_id = lax.broadcasted_iota(jnp.int32, (STEP, LANE), 1).astype(F32)

    def base_of(b):
        return pl.multiple_of(b * STEP, STEP)

    def member(base):
        return S.seg[pl.ds(base + RIM, STEP), :] == lane_id

    def table_add(onehot, v):
        return fold(jnp.where(onehot, jnp.sum(v, axis=1, keepdims=True), 0.0))

    def pick(onehot, row):
        return jnp.sum(jnp.where(onehot, row, 0.0), axis=1, keepdims=True)

    zero_tab = jnp.zeros((8, LANE), F32)

    def send_table(rnd, t1, t2):
        row = lax.broadcasted_iota(jnp.int32, (8, LANE), 0)
        t1 = jnp.sum(t1, axis=0, keepdims=True)
        t2 = jnp.sum(t2, axis=0, keepdims=True)
        S.tab[rnd] = jnp.where(row == 0, t1, jnp.where(row == 1, t2, 0.0))
        return [
            push(S.tab.at[rnd], S.tabr.at[rnd, n], S.ts.at[rnd, n], S.tr.at[rnd, n], along(s, core[rel]))
            for n, (s, rel) in enumerate(OFFSETS)
        ]

    def take_table(rnd, copies):
        total = S.tab[rnd]
        for copy in copies:
            copy.wait_recv()
        for n in range(9):
            total = total + S.tabr[rnd, n]
        count = S.cnt[0:1, :]
        return total[0:1] / count, total[1:2] / count

    def inside_first(step, carry, then):
        carry = lax.fori_loop(1, steps - 1, step, carry)
        then()
        return lax.fori_loop(0, 2, lambda b, held: step(b * (steps - 1), held), carry)

    def conv_forward(s, copies):
        def step(b, carry):
            t1, t2 = carry
            base = base_of(b)
            centre = S.seg[pl.ds(base + RIM, STEP), :]
            first = second = jnp.zeros((STEP, LANE), F32)
            for g in range(0, TILES, GROUP):
                acc = [jnp.zeros((STEP, LANE), F32) for _ in range(GROUP)]
                for j in range(TAPS):
                    same = S.seg[pl.ds(base + j + 1, STEP), :] == centre
                    for c in range(GROUP):
                        window = S.xf[s, g + c, pl.ds(base + j + 1, STEP), :]
                        acc[c] = acc[c] + jnp.where(same, window * S.pb[s, g + c, j : j + 1, :], 0.0)
                for c in range(GROUP):
                    S.y[s, g + c, pl.ds(base + RIM, STEP), :] = acc[c]
                    first = first + acc[c]
                    second = second + acc[c] * acc[c]
            onehot = member(base)
            return t1 + table_add(onehot, first), t2 + table_add(onehot, second)

        return inside_first(step, (zero_tab, zero_tab), lambda: take_halo(s, copies, S.xf.at[s]))

    def moments(rnd, copies):
        mean, square = take_table(rnd, copies)
        spread = jnp.maximum(square - mean * mean, 0.0)
        return mean, lax.rsqrt(spread + EPSILON)

    def normalize(s, base, onehot, mean, scale):
        m, v = pick(onehot, mean), pick(onehot, scale)
        S.inv[s, pl.ds(base, STEP), :] = jnp.broadcast_to(v, (STEP, LANE))
        return m, v

    def activate(s, base, c, normed):
        gain, bias = S.pb[s, c, TAPS : TAPS + 1, :], S.pb[s, c, TAPS + 1 : TAPS + 2, :]
        pre = normed * gain + bias
        sig = jax.nn.sigmoid(pre)
        return gain, pre, sig

    def act_grad(s):
        S.ag[s] = dot_t(S.gbuf[s, 0], S.w[s, :, 0:HALF]) + dot_t(S.gbuf[s, 1], S.w[s, :, HALF:])

    def pre_grad(s, mean, scale):
        def step(b, carry):
            t1, t2, gains, biases = carry
            base = base_of(b)
            onehot = member(base)
            at = pl.ds(base, STEP)
            if s == 1:
                m, v = normalize(1, base, onehot, mean, scale)
            first = second = jnp.zeros((STEP, LANE), F32)
            new_gains, new_biases = [], []
            for c in range(TILES):
                if s == 1:
                    normed = (S.y[1, c, pl.ds(base + RIM, STEP), :] - m) * v
                    S.nrm[1, c, at, :] = normed
                else:
                    normed = S.nrm[0, c, at, :]
                gain, pre, sig = activate(s, base, c, normed)
                if s == 1:
                    S.act[1, at, cols(c)] = (pre * sig).astype(BF16)
                grad = S.ag[s, at, cols(c)] * sig * (1.0 + pre * (1.0 - sig))
                scaled = grad * gain
                S.ag[s, at, cols(c)] = scaled
                if s == 1:
                    S.cg[c, pl.ds(base + RIM, STEP), :] = scaled
                first = first + scaled
                second = second + scaled * normed
                new_gains.append(gains[c] + fold(grad * normed))
                new_biases.append(biases[c] + fold(grad))
            return (t1 + table_add(onehot, first), t2 + table_add(onehot, second),
                    tuple(new_gains), tuple(new_biases))

        zeros = tuple(zero_tab for _ in range(TILES))
        t1, t2, gains, biases = lax.fori_loop(0, steps, step, (zero_tab, zero_tab, zeros, zeros))
        for c in range(TILES):
            S.gba[s, 0, c] = gains[c]
            S.gba[s, 1, c] = biases[c]
        return t1, t2

    def conv_grad(s, mean_a, mean_b):
        def step(b, _):
            base = base_of(b)
            onehot = member(base)
            ca, cb = pick(onehot, mean_a), pick(onehot, mean_b)
            at = pl.ds(base, STEP)
            v = S.inv[s, at, :]
            for c in range(TILES):
                S.cg[c, pl.ds(base + RIM, STEP), :] = v * (S.ag[s, at, cols(c)] - ca - S.nrm[s, c, at, :] * cb)
            return 0

        lax.fori_loop(0, steps, step, 0)

    def send_edges(rnd, k, src):
        for c in range(TILES):
            S.edge[k, 0, :, cols(c)] = src[c, RIM : 2 * RIM, :].astype(BF16)
            S.edge[k, 1, :, cols(c)] = src[c, ROWS : ROWS + RIM, :].astype(BF16)
        return send_halo(rnd, S.edge.at[k, 0], S.edge.at[k, 1])

    def back_step(k, src):
        def step(b, _):
            base = base_of(b)
            centre = S.seg[pl.ds(base + RIM, STEP), :]
            for g in range(0, TILES, GROUP):
                acc = [jnp.zeros((STEP, LANE), F32) for _ in range(GROUP)]
                for j in range(TAPS):
                    same = S.seg[pl.ds(base + TAPS - 1 - j, STEP), :] == centre
                    for c in range(GROUP):
                        term = S.pb[1, g + c, j : j + 1, :]
                        if src is not None:
                            term = src[g + c, pl.ds(base + TAPS - 1 - j, STEP), :] * term
                        acc[c] = acc[c] + jnp.where(same, term, 0.0)
                for c in range(GROUP):
                    S.cb[k, g + c, pl.ds(base, STEP), :] = acc[c]
            return 0

        return step

    def back_inner(k, src):
        lax.fori_loop(1, steps - 1, back_step(k, src), 0)

    def back_outer(k, src):
        lax.fori_loop(0, 2, lambda b, _: back_step(k, src)(b * (steps - 1), 0), 0)

    def pass_down(mean, mean_a, mean_b):
        def step(b, _):
            base = base_of(b)
            onehot = member(base)
            at = pl.ds(base, STEP)
            v = S.inv[1, at, :]
            slope = pick(onehot, mean_b) * v
            level = pick(onehot, mean_a) - slope * pick(onehot, mean)
            for c in range(TILES):
                back = v * (S.cb[2, c, at, :] - level * S.cb[0, c, at, :] - slope * S.cb[1, c, at, :])
                S.gbuf[0, p, at, cols(c)] = (S.gbuf[1, p, at, cols(c)].astype(F32) + back).astype(BF16)
            return 0

        lax.fori_loop(0, steps, step, 0)

    def conv_backward(s, then):
        def step(b, _):
            base = base_of(b)
            at = pl.ds(base, STEP)
            centre = S.seg[pl.ds(base + RIM, STEP), :]
            for g in range(0, TILES, GROUP):
                acc = [jnp.zeros((STEP, LANE), F32) for _ in range(GROUP)]
                for j in range(TAPS):
                    same = S.seg[pl.ds(base + TAPS - 1 - j, STEP), :] == centre
                    for c in range(GROUP):
                        window = S.cg[g + c, pl.ds(base + TAPS - 1 - j, STEP), :]
                        acc[c] = acc[c] + jnp.where(same, window * S.pb[s, g + c, j : j + 1, :], 0.0)
                for c in range(GROUP):
                    passed = S.gbuf[s, p, at, cols(g + c)].astype(F32) + acc[c]
                    gi_ref[0, at, cols(g + c)] = passed.astype(BF16)
            return 0

        inside_first(step, 0, then)

    def kernel_grad(s, low, high):
        def step(b, _):
            base = base_of(b)
            centre = S.seg[pl.ds(base + RIM, STEP), :]
            for g in range(0, TILES, GROUP):
                mine = [S.cg[g + c, pl.ds(base + RIM, STEP), :] for c in range(GROUP)]
                for j in range(TAPS):
                    same = S.seg[pl.ds(base + j + 1, STEP), :] == centre
                    for c in range(GROUP):
                        window = S.xf[s, g + c, pl.ds(base + j + 1, STEP), :]
                        S.kga[s, g + c, j] += fold(jnp.where(same, window * mine[c], 0.0))
            return 0

        lax.fori_loop(low, high, step, 0)

    def keep_small(s):
        row = lax.broadcasted_iota(jnp.int32, (8, LANE), 0)
        for c in range(TILES):
            for k in range(4):
                t = c * 5 + k
                at = slice(s * 16 + (t % 2) * 8, s * 16 + (t % 2) * 8 + 8)
                S.sb[t // 2, at, :] = jnp.sum(S.kga[s, c, 8 * k : 8 * k + 8], axis=1)
            t = c * 5 + 4
            at = slice(s * 16 + (t % 2) * 8, s * 16 + (t % 2) * 8 + 8)
            gsum = jnp.sum(S.gba[s, 0, c], axis=0, keepdims=True)
            bsum = jnp.sum(S.gba[s, 1, c], axis=0, keepdims=True)
            S.sb[t // 2, at, :] = jnp.where(row == 0, gsum, jnp.where(row == 1, bsum, 0.0))

    q1, q2 = HALF // 4, HALF // 16
    first_place = jnp.where(p == 0, y, x)
    second_place = jnp.where(p == 0, x, y)

    def first_ring(d, path):
        return plane(d * path, d * (1 - path), path)

    def second_ring(d):
        return plane(d * (1 - p), d * p, p)

    def send_cotangent(s, distances):
        return [
            push(S.gbuf.at[s, p], S.gq.at[s, d - 1], S.gqs.at[s, d - 1], S.gqr.at[s, d - 1], first_ring(d, p))
            for d in distances
        ]

    def forward_cotangent(s):
        half = ROWS // 2
        return [
            push(
                S.gq.at[s, d - 1, pl.ds(at, half), :], S.gq.at[s, 1, pl.ds(at, half), :],
                S.gqs.at[s, n], S.gqr.at[s, n], first_ring(d, p),
            )
            for d, at, n in ((1, 0, 1), (3, half, 3))
        ]

    def turn_activation(s):
        def step(k, _):
            at = pl.ds(pl.multiple_of(k * 256, 256), 256)
            for path in range(2):
                S.turn[s, path, at, :] = dot_t(S.perm[path, at, :], S.act[s]).astype(BF16)
            return 0

        lax.fori_loop(0, HALF // 256, step, 0)

    def push_activation(s):
        copies = []
        for d in range(4):
            for rel in range(2):
                path = core[rel]
                place = lax.rem(jnp.where(path == 0, y, x) + d, 4)
                rows = pl.ds(pl.multiple_of(place * q1, q1), q1)
                if (d, rel) == (0, 0):
                    S.ta[s, 0, p] = S.turn[s, p, rows, :]
                else:
                    copies.append(push(
                        S.turn.at[s, path, rows, :], S.ta.at[s, d, p], S.tas.at[s, d, rel], S.tar.at[s, d, rel],
                        first_ring(d, path),
                    ))
        return copies

    def first_sum(s, copies):
        for copy in copies:
            copy.wait_recv()
        for h in range(2):
            total = dot(S.ta[s, 0, h], S.gbuf[s, p])
            for d in range(3):
                total = total + dot(S.ta[s, d + 1, h], S.gq[s, d])
            S.s2[s, h] = total.astype(BF16)
        return [
            push(
                S.s2.at[s, :, pl.ds(pl.multiple_of(lax.rem(second_place + d, 4) * q2, q2), q2), :],
                S.r2.at[s, d - 1], S.s2s.at[s, d - 1], S.s2r.at[s, d - 1], second_ring(d),
            )
            for d in (1, 3, 2)
        ]

    def third_copy(s, dz):
        rel = jnp.where(p == s, 0, 1)
        return pltpu.make_async_remote_copy(
            src_ref=S.s3.at[s, lax.rem(z + dz, NZ)], dst_ref=S.r3.at[dz, rel], send_sem=S.s3s.at[s, dz],
            recv_sem=S.s3r.at[dz, rel], device_id=depth(dz, s), device_id_type=MESH,
        )

    def second_sum(s, copies):
        for copy in copies:
            copy.wait_recv()
        mine = pl.ds(pl.multiple_of(second_place * q2, q2), q2)
        for h in range(2):
            total = S.s2[s, h, mine, :].astype(F32)
            for d in range(3):
                total = total + S.r2[s, d, h].astype(F32)
            S.t3[0:q2, :] = total
            for k in range(4):
                S.s3[s, 4 * h + k] = S.t3[BLOCK * k : BLOCK * k + 16, :].astype(BF16)
        for dz in DEPTH:
            third_copy(s, dz).start()

        @pl.when(p != s)
        def _():
            third_copy(s, 0).start()

        @pl.when(p == s)
        def _():
            S.r3[0, 0] = S.s3[s, z]

    def third_sum():
        for s in range(2):
            for dz in range(1, NZ):
                third_copy(s, dz).wait_send()

            @pl.when(p != s)
            def _():
                third_copy(s, 0).wait_send()
        for rel, at in ((0, own_col), (1, oth_col)):
            total = jnp.zeros((16, HALF), F32)
            for dz in range(NZ):
                if (dz, rel) != (0, 0):
                    pltpu.make_async_remote_copy(
                        src_ref=S.s3.at[0, 0], dst_ref=S.r3.at[dz, rel], send_sem=S.s3s.at[0, 0],
                        recv_sem=S.s3r.at[dz, rel], device_id=along(0, q), device_id_type=MESH,
                    ).wait_recv()
                total = total + S.r3[dz, rel].astype(F32)
            for k in range(BLOCK):
                gw_ref[k, :, pl.ds(at, HALF)] = total[k : k + 1]

    loc[2].wait()
    loc[3].wait()
    cotangent1 = send_cotangent(1, (2,))
    par_copy.wait_recv()
    copies = send_table(0, *conv_forward(0, halo_copies))
    lax.fori_loop(0, steps, back_step(0, None), 0)
    loc[1].wait()
    w_copy.wait_recv()
    act_grad(1)
    mean, scale = moments(0, copies)
    cotangent1 += send_cotangent(1, (1, 3))

    def norm_step(b, _):
        base = base_of(b)
        m, v = normalize(0, base, member(base), mean, scale)
        for c in range(TILES):
            normed = (S.y[0, c, pl.ds(base + RIM, STEP), :] - m) * v
            S.nrm[0, c, pl.ds(base, STEP), :] = normed
            _, pre, sig = activate(0, base, c, normed)
            S.act[0, pl.ds(base, STEP), cols(c)] = (pre * sig).astype(BF16)
        return 0

    lax.fori_loop(0, steps, norm_step, 0)
    S.hx[0] = dot(S.act[0], S.w[0, :, pl.ds(oth_col, HALF)]).astype(BF16)
    copy = push(S.hx.at[0], S.hx.at[1], S.xs.at[0], S.xr.at[0], along(0, q))
    S.part[...] = dot(S.act[0], S.w[0, :, pl.ds(own_col, HALF)])
    turn_activation(0)
    copy.wait_recv()

    def out_step(b, _):
        base = base_of(b)
        at = pl.ds(base, STEP)
        S.h1[at, :] = (S.hb[at, :].astype(F32) + (S.part[at, :] + S.hx[1, at, :].astype(F32))).astype(BF16)
        return 0

    lax.fori_loop(0, steps, out_step, 0)
    halo_copies = send_halo(1, S.h1.at[pl.ds(0, RIM), :], S.h1.at[pl.ds(ROWS - RIM, RIM), :])
    for c in range(TILES):
        S.xf[1, c, RIM : RIM + ROWS, :] = S.h1[:, cols(c)].astype(F32)

    copies = send_table(1, *conv_forward(1, halo_copies))

    halo_y = send_edges(4, 2, S.y.at[1])
    activation0 = push_activation(0)
    back_inner(1, S.y.at[1])
    mean, scale = moments(1, copies)

    copies = send_table(2, *pre_grad(1, mean, scale))
    halo_n = send_edges(2, 1, S.cg)
    back_inner(2, S.cg)
    take_halo(4, halo_y, S.y.at[1])
    back_outer(1, S.y.at[1])
    take_halo(2, halo_n, S.cg)
    back_outer(2, S.cg)
    mean_a, mean_b = take_table(2, copies)
    pass_down(mean, mean_a, mean_b)
    copy = push(S.gbuf.at[0, p], S.gbuf.at[0, p], S.xs.at[1], S.xr.at[1], along(0, q))
    cotangent0 = send_cotangent(0, (1, 3))
    turn_activation(1)
    copy.wait_recv()

    act_grad(0)
    copies = send_table(3, *pre_grad(0, None, None))
    activation1 = push_activation(1)
    conv_grad(1, mean_a, mean_b)
    kernel_grad(1, 0, steps)
    keep_small(1)
    mean_a, mean_b = take_table(3, copies)
    conv_grad(0, mean_a, mean_b)
    halo_copies = send_edges(3, 0, S.cg)
    for copy in cotangent0:
        copy.wait_recv()
    cotangent0 = forward_cotangent(0)
    kernel_grad(0, 0, steps)
    keep_small(0)

    place = x * NY + y
    small = [
        push(
            S.sb.at[lax.rem(x + dx, NX) * NY + lax.rem(y + dy, NY)], S.ar.at[n],
            S.as_.at[n], S.ar_.at[n], plane(dx, dy, p),
        )
        for n, (dx, dy) in enumerate(PLANE[:-1])
    ]
    second1 = first_sum(1, activation1 + cotangent1)
    second0 = first_sum(0, activation0 + cotangent0)
    conv_backward(0, lambda: take_halo(3, halo_copies, S.cg))
    for copy in small:
        copy.wait_recv()
    total = S.sb[place]
    for n in range(15):
        total = total + S.ar[n]
    S.zb[z] = total
    small = [
        push(S.zb.at[z], S.zb.at[z], S.zs.at[dz - 1], S.zr.at[dz - 1], depth(dz, p))
        for dz in DEPTH
    ]
    second_sum(1, second1)
    second_sum(0, second0)
    for dz in range(1, NZ):
        from_z = lax.rem(z + NZ - dz, NZ)
        pltpu.make_async_remote_copy(
            src_ref=S.zb.at[from_z], dst_ref=S.zb.at[from_z], send_sem=S.zs.at[dz - 1],
            recv_sem=S.zr.at[dz - 1], device_id=depth(dz, p), device_id_type=MESH,
        ).wait_recv()
    total = S.zb[0]
    for k in range(1, NZ):
        total = total + S.zb[k]
    S.fs[0] = total[0:16]
    S.fs[1] = total[16:32]
    S.fin[p, place] = S.fs[p]
    small = [
        push(S.fs.at[core[rel]], S.fin.at[p, place], S.gs.at[n], S.gr.at[n], plane(dx, dy, core[rel]))
        for n, (dx, dy, rel) in enumerate(GATHER)
    ]
    third_sum()
    for copy in small:
        copy.wait_recv()
    for h in range(2):
        for c in range(TILES):
            at = slice(h * HALF + c * LANE, h * HALF + (c + 1) * LANE)
            for k in range(4):
                t = c * 5 + k
                gk_ref[0, 8 * k : 8 * k + 8, at] = S.fin[h, t // 2, (t % 2) * 8 : (t % 2) * 8 + 8, :]
            t = c * 5 + 4
            gg_ref[:, at] = S.fin[h, t // 2, (t % 2) * 8 : (t % 2) * 8 + 1, :]
            gb_ref[:, at] = S.fin[h, t // 2, (t % 2) * 8 + 1 : (t % 2) * 8 + 2, :]
    for copy in sends:
        copy.wait_send()


def relay_kernel(*refs):
    for k in range(5):
        refs[5 + k][...] = refs[k][...]


def body(*args):
    shapes = scratch()
    names = list(shapes)
    vmem, hbm = pl.BlockSpec(memory_space=pltpu.VMEM), pl.BlockSpec(memory_space=pl.ANY)

    def kern(*refs):
        main_kernel(names, *refs)

    results = pl.pallas_call(
        kern,
        out_shape=(
            jax.ShapeDtypeStruct((1, ROWS, HALF), BF16),
            jax.ShapeDtypeStruct((BLOCK, 1, D), F32),
            jax.ShapeDtypeStruct((1, TAPS, D), F32),
            jax.ShapeDtypeStruct((1, D), F32),
            jax.ShapeDtypeStruct((1, D), F32),
        ),
        in_specs=[hbm, hbm, vmem, hbm, vmem, vmem, vmem],
        out_specs=[vmem] * 5,
        scratch_shapes=list(shapes.values()),
        compiler_params=pltpu.CompilerParams(
            collective_id=0, has_side_effects=True, vmem_limit_bytes=56 << 20
        ),
    )(*args)
    gi, gw, gk, gg, gb = pl.pallas_call(
        relay_kernel,
        out_shape=tuple(jax.ShapeDtypeStruct(r.shape, r.dtype) for r in results),
        in_specs=[vmem] * 5,
        out_specs=[vmem] * 5,
    )(*results)
    return gi, gw.reshape(1, BLOCK, D), gk, gg, gb


def solution(mesh):
    return jax.shard_map(
        body,
        mesh=mesh,
        in_specs=(
            P("dp", "seq", None),
            P("dp", "seq", None),
            P("dp", None),
            P("pipe", None, None),
            P("pipe", None, None),
            P("pipe", None),
            P("pipe", None),
        ),
        out_specs=(
            P("dp", "seq", "pipe"),
            P("pipe", ("seq", "dp"), None),
            P("pipe", None, None),
            P("pipe", None),
            P("pipe", None),
        ),
        check_vma=False,
    )
```
